128 devices in a mesh: ctx: 32 (over y, z, core), head: 4 (over x).
Axes of the slice: x: 4, y: 4, z: 4, core: 2. Of those that a mesh axis runs over, the one named last changes fastest.
Arguments:
- queries: bfloat16 [65536, 512], P(('ctx', 'head')), may hold values from -6 to 6
- keys: bfloat16 [65536, 512], P(('ctx', 'head')), may hold values from -6 to 6
- values: bfloat16 [65536, 512], P(('ctx', 'head')), may hold values from -6 to 6
- output: bfloat16 [65536, 512], P(('ctx', 'head')), may hold values from -3 to 3
- out_grad: bfloat16 [65536, 512], P(('ctx', 'head')), may hold values from -6 to 6
- slopes: float32 [4], replicated, may hold values from 4.8828124e-06 to 0.000390625
- windows: int32 [4], replicated, may hold values from 2048 to 6144, as said below
Outputs:
- query_grad: bfloat16 [65536, 512], P(('ctx', 'head'))
- key_grad: bfloat16 [65536, 512], P(('ctx', 'head'))
- value_grad: bfloat16 [65536, 512], P(('ctx', 'head'))
The draws below stay inside these ranges and needn't reach their ends.
Inputs may be any that keep to these rules, and one draw needn't show every extreme that they name: `windows`: each window is a multiple of 2048; some head has exactly 6144.
All inputs are finite; a program needn't handle non-finite values.
Results may differ from the reference program's by a relative error of at most 0.012.
Values may be sent and summed in bfloat16 or wider, within the bound.
A program may use at most 128 MiB of HBM per device.

```python
import math
import jax
import jax.numpy as jnp
from jax import lax

HEAD_DIM = 128
TOK_DEV = 2048
MAXHOPS = 3
HEADS = 4
SEQ = 65536
N_CTX = 32


QUERY_LEVEL = 5.875


def alignment(key):
    key = jax.random.fold_in(key, 101)
    first, second, third, fourth = jax.random.split(key, 4)
    blocks = SEQ // TOK_DEV
    offsets = jax.random.randint(first, (blocks,), 2, TOK_DEV)
    ranks = jax.random.permutation(second, blocks).astype(jnp.float32)
    target = 120.0 + 140.0 * ranks / max(blocks - 1, 1)
    spacing = jax.random.uniform(third, (blocks,), minval=1.0, maxval=3.0)
    signs = jnp.where(jax.random.bernoulli(fourth, 0.5, (HEADS * HEAD_DIM,)), 1.0, -1.0)
    rows = (jnp.arange(blocks) * TOK_DEV + offsets).astype(jnp.int32)
    return (rows, target, spacing, signs)


def draw_queries(key, part):
    rows, target, spacing, signs = alignment(key)
    key = jax.random.fold_in(key, 23)
    first = jax.random.fold_in(key, 0)
    base = jnp.clip(1.5 * jax.random.normal(first, (SEQ, HEADS * HEAD_DIM)), -6.0, 6.0)
    base = base.at[rows].set(QUERY_LEVEL * signs[None, :])
    return base.astype(jnp.bfloat16)


def draw_keys(key, part):
    rows, target, spacing, signs = alignment(key)
    key = jax.random.fold_in(key, 29)
    first = jax.random.fold_in(key, 0)
    base = jnp.clip(1.5 * jax.random.normal(first, (SEQ, HEADS * HEAD_DIM)), -6.0, 6.0)
    level = jnp.minimum(target / (QUERY_LEVEL * math.sqrt(HEAD_DIM)), 5.9)
    lowered = spacing * math.sqrt(HEAD_DIM) / (4.0 * QUERY_LEVEL)
    columns = jnp.arange(HEADS * HEAD_DIM) % HEAD_DIM
    nearest = level[:, None] * signs[None, :]
    second_row = jnp.where(columns[None, :] < 4, (level - lowered)[:, None], level[:, None]) * signs[None, :]
    base = base.at[rows - 1].set(nearest).at[rows - 2].set(second_row)
    return base.astype(jnp.bfloat16)


def draw_windows(key, part):
    key = jax.random.fold_in(key, 11)
    first, second = jax.random.split(key)
    blocks = jax.random.randint(first, (HEADS,), 1, MAXHOPS + 1)
    chosen = jax.random.randint(second, (), 0, HEADS)
    blocks = jnp.where(jnp.arange(HEADS) == chosen, MAXHOPS, blocks)
    return (blocks * TOK_DEV).astype(jnp.int32)


def steps_of(own_key, shape, pieces, least, largest):
    gain = 1.0
    for position, parts in pieces:
        heights = jax.random.uniform(jax.random.fold_in(jax.random.fold_in(own_key, 6), position), (parts,), jnp.float32, least / len(pieces), largest / len(pieces))
        gain = gain * jnp.repeat(jnp.exp(heights), shape[position] // parts).reshape((-1,) + (1,) * (len(shape) - 1 - position))
    return gain


def bell_draw(own_key, shape, spread, reach, cuts=(), kind=jnp.bfloat16):
    values = spread * jax.random.normal(own_key, shape, jnp.float32)
    if cuts:
        values = values * steps_of(own_key, shape, cuts, -0.22, 0.18)
    return jnp.clip(values, -reach, reach).astype(kind)


def setup_inputs(seed: int = 0) -> dict:
    streams_of = jax.random.split(jax.random.key(seed), 8)
    return {
        "queries": draw_queries(jax.random.fold_in(streams_of[7], 71), 0),
        "keys": draw_keys(jax.random.fold_in(streams_of[7], 71), 0),
        "values": bell_draw(streams_of[2], (SEQ, HEADS * HEAD_DIM), 1.0, 6.0, ((0, 128),)),
        "output": bell_draw(streams_of[3], (SEQ, HEADS * HEAD_DIM), 0.5, 3.0, ((0, 128),)),
        "out_grad": bell_draw(streams_of[4], (SEQ, HEADS * HEAD_DIM), 1.0, 6.0, ((0, 128),)),
        "slopes": jnp.clip(jnp.exp(jax.random.uniform(streams_of[5], (HEADS,), jnp.float32, math.log(4.882812390860636e-06), math.log(0.000390625))), 4.882812390860636e-06, 0.000390625),
        "windows": draw_windows(jax.random.fold_in(streams_of[7], 71), 0),
    }


def block_scores(query_rows, key_rows, query_pos, key_pos, slopes, windows):
    rows = query_rows.shape[0]
    cols = key_rows.shape[0]
    query_heads = query_rows.astype(jnp.float32).reshape(rows, HEADS, HEAD_DIM)
    key_heads = key_rows.astype(jnp.float32).reshape(cols, HEADS, HEAD_DIM)
    scores = jnp.einsum('qhd,khd->hqk', query_heads, key_heads) * (HEAD_DIM ** -0.5)
    distance = query_pos[:, None] - key_pos[None, :]
    scores = scores - slopes[:, None, None] * distance.astype(jnp.float32)[None]
    inside = (distance >= 0)[None] & (distance[None] < windows[:, None, None])
    inside = inside & (key_pos >= 0)[None, None, :] & (query_pos < SEQ)[None, :, None]
    return scores, inside


def to_heads(rows):
    return rows.astype(jnp.float32).reshape(rows.shape[0], HEADS, HEAD_DIM)


def reference(queries, keys, values, output, out_grad, slopes, windows):
    scale_factor = HEAD_DIM ** -0.5
    front = MAXHOPS * TOK_DEV
    span = (MAXHOPS + 1) * TOK_DEV
    delta = jnp.sum(to_heads(out_grad) * to_heads(output), axis=2).T
    keys_pad = jnp.pad(keys, ((front, 0), (0, 0)))
    values_pad = jnp.pad(values, ((front, 0), (0, 0)))

    def query_block(block):
        start = (block * TOK_DEV).astype(jnp.int32)
        query_rows = lax.dynamic_slice_in_dim(queries, start, TOK_DEV, 0)
        grad_rows = lax.dynamic_slice_in_dim(out_grad, start, TOK_DEV, 0)
        key_rows = lax.dynamic_slice_in_dim(keys_pad, start, span, 0)
        value_rows = lax.dynamic_slice_in_dim(values_pad, start, span, 0)
        delta_rows = lax.dynamic_slice_in_dim(delta, start, TOK_DEV, 1)
        query_pos = start + jnp.arange(TOK_DEV, dtype=jnp.int32)
        key_pos = start - front + jnp.arange(span, dtype=jnp.int32)
        scores, inside = block_scores(query_rows, key_rows, query_pos, key_pos, slopes, windows)
        top = jnp.max(jnp.where(inside, scores, -1e30), axis=2, keepdims=True)
        total = jnp.sum(jnp.where(inside, jnp.exp(scores - top), 0.0), axis=2, keepdims=True)
        lse = top + jnp.log(total)
        prob = jnp.where(inside, jnp.exp(scores - lse), 0.0)
        dprob = jnp.einsum('qhd,khd->hqk', to_heads(grad_rows), to_heads(value_rows))
        dscore = (prob * (dprob - delta_rows[:, :, None])).astype(jnp.bfloat16)
        dscore = lax.optimization_barrier(dscore).astype(jnp.float32)
        query_part = jnp.einsum('hqk,khd->qhd', dscore, to_heads(key_rows)) * scale_factor
        return query_part.reshape(TOK_DEV, HEADS * HEAD_DIM).astype(jnp.bfloat16), lse[:, :, 0]

    query_grad, lse_blocks = lax.map(query_block, jnp.arange(N_CTX, dtype=jnp.int32))
    query_grad = query_grad.reshape(SEQ, HEADS * HEAD_DIM)
    lse_all = jnp.transpose(lse_blocks, (1, 0, 2)).reshape(HEADS, SEQ)
    queries_pad = jnp.pad(queries, ((0, front), (0, 0)))
    grads_pad = jnp.pad(out_grad, ((0, front), (0, 0)))
    lse_pad = jnp.pad(lse_all, ((0, 0), (0, front)))
    delta_pad = jnp.pad(delta, ((0, 0), (0, front)))

    def key_block(block):
        start = (block * TOK_DEV).astype(jnp.int32)
        key_rows = lax.dynamic_slice_in_dim(keys, start, TOK_DEV, 0)
        value_rows = lax.dynamic_slice_in_dim(values, start, TOK_DEV, 0)
        query_rows = lax.dynamic_slice_in_dim(queries_pad, start, span, 0)
        grad_rows = lax.dynamic_slice_in_dim(grads_pad, start, span, 0)
        lse_rows = lax.dynamic_slice_in_dim(lse_pad, start, span, 1)
        delta_rows = lax.dynamic_slice_in_dim(delta_pad, start, span, 1)
        query_pos = start + jnp.arange(span, dtype=jnp.int32)
        key_pos = start + jnp.arange(TOK_DEV, dtype=jnp.int32)
        scores, inside = block_scores(query_rows, key_rows, query_pos, key_pos, slopes, windows)
        prob = jnp.where(inside, jnp.exp(scores - lse_rows[:, :, None]), 0.0)
        dprob = jnp.einsum('qhd,khd->hqk', to_heads(grad_rows), to_heads(value_rows))
        dscore = (prob * (dprob - delta_rows[:, :, None])).astype(jnp.bfloat16)
        dscore = lax.optimization_barrier(dscore).astype(jnp.float32)
        prob_half = lax.optimization_barrier(prob.astype(jnp.bfloat16)).astype(jnp.float32)
        key_part = jnp.einsum('hqk,qhd->khd', dscore, to_heads(query_rows)) * scale_factor
        value_part = jnp.einsum('hqk,qhd->khd', prob_half, to_heads(grad_rows))
        return (key_part.reshape(TOK_DEV, HEADS * HEAD_DIM).astype(jnp.bfloat16),
                value_part.reshape(TOK_DEV, HEADS * HEAD_DIM).astype(jnp.bfloat16))

    key_grad, value_grad = lax.map(key_block, jnp.arange(N_CTX, dtype=jnp.int32))
    return (query_grad, key_grad.reshape(SEQ, HEADS * HEAD_DIM), value_grad.reshape(SEQ, HEADS * HEAD_DIM))
```

```python
import functools
import math

import jax
import jax.numpy as jnp
from jax import lax
from jax.experimental import pallas as pl
from jax.experimental.pallas import tpu as pltpu
from jax.sharding import PartitionSpec as P

D = 128
SCALE = D ** (-0.5)
LOG2E = math.log2(math.e)
TO_LOG2 = SCALE * LOG2E
BIG = 1e30
F32 = jnp.float32
BF16 = jnp.bfloat16
MESH = pl.DeviceIdType.MESH
SUBS = 4
NT_DIMS = (((1,), (1,)), ((), ()))
TN_DIMS = (((0,), (0,)), ((), ()))

A, B, C, DD = range(4)
QSLOT = (0, 1, 1, 2)
KSLOT = (0, 0, 1, 1)


def kernel(
    n_ctx,
    n_head,
    slopes,
    windows,
    q_in,
    k_in,
    v_in,
    o_in,
    g_in,
    dq_out,
    dk_out,
    dv_out,
    qx,
    kx,
    gb,
    vb,
    ov,
    gv,
    p_ad,
    p_b,
    p_c,
    stat,
    ratio,
    dqt,
    dka,
    dva,
    delta_out,
    delta_in,
    part_out,
    part_in,
    ret_out,
    ret_in,
    dq_send,
    dq_recv,
    dkv_send,
    dkv_recv,
    fin,
    x_ssem,
    x_rsem,
    h_ssem,
    h_rsem,
    d_ssem,
    d_rsem,
    s_ssem,
    s_rsem,
    dq_ssem,
    dq_rsem,
    kv_ssem,
    kv_rsem,
    o_ssem,
    o_rsem,
    l_sem,
):
    ch = q_in.shape[0]
    n = n_head * ch
    sub = ch // SUBS
    ctx = lax.axis_index("ctx")
    me = lax.axis_index("head")
    odd = lax.rem(ctx, 2)
    partner = ctx + 1 - 2 * odd

    def along(by):
        return (lax.rem(ctx + by + n_ctx, n_ctx), me)

    def peer(by):
        return lax.rem(me + by, n_head)

    def rows(j):
        return pl.ds(pl.multiple_of(j * ch, ch), ch)

    def lanes(j):
        return pl.ds(pl.multiple_of(j * D, D), D)

    def remote(src, dst, ssem, rsem, device):
        return pltpu.make_async_remote_copy(
            src_ref=src, dst_ref=dst, send_sem=ssem, recv_sem=rsem,
            device_id=device, device_id_type=MESH,
        )

    sends = []

    def send(src, dst, ssem, rsem, device):
        copy = remote(src, dst, ssem, rsem, device)
        copy.start()
        sends.append(copy)

    def arrived(dst, ssem, rsem):
        remote(dst, dst, ssem, rsem, along(0)).wait_recv()

    slope = slopes[me]
    window = windows[me]

    bufs = (qx, kx, gb, vb)
    ins = (q_in, k_in, g_in, v_in)

    def chunk(a, slot, j):
        if a < 2:
            return bufs[a].at[slot, rows(j), 0:D]
        return bufs[a].at[slot, rows(j), :]

    own = []
    for a in range(4):
        copy = pltpu.make_async_copy(ins[a].at[:, lanes(me)], chunk(a, 0, me), x_rsem.at[a, me])
        copy.start()
        own.append(copy)
    copy_o = pltpu.make_async_copy(o_in, ov, l_sem.at[0])
    copy_g = pltpu.make_async_copy(g_in, gv, l_sem.at[1])
    copy_o.start()
    copy_g.start()

    barrier = pltpu.get_barrier_semaphore()
    neighbours = [along(1), along(-1), along(2), along(-2)]
    neighbours += [(ctx, peer(by)) for by in range(1, n_head)]
    for device in neighbours:
        pl.semaphore_signal(barrier, inc=1, device_id=device, device_id_type=MESH)
    pl.semaphore_wait(barrier, len(neighbours))

    for a in range(4):
        for by in (1, 3, 2):
            to = peer(by)
            send(ins[a].at[:, lanes(to)], chunk(a, 0, me), x_ssem.at[a, by], x_rsem.at[a, me], (ctx, to))

    lane = lax.broadcasted_iota(jnp.int32, (1, D), 1)
    ones = jnp.broadcast_to(jnp.where(lane < 3, 1.0, 0.0), (ch, D)).astype(BF16)

    def fill(t, _):
        for slot in range(3):
            qx[slot, rows(t), D:] = ones
        pos = (lax.broadcasted_iota(jnp.int32, (ch, D), 0) + t * ch).astype(F32)
        bias = pos * (slope / SCALE)
        high = bias.astype(BF16).astype(F32)
        mid = (bias - high).astype(BF16).astype(F32)
        low = bias - high - mid
        terms = jnp.where(lane == 0, high, jnp.where(lane == 1, mid, jnp.where(lane == 2, low, 0.0)))
        for slot in range(2):
            kx[slot, rows(t), D:] = terms.astype(BF16)
        return 0

    lax.fori_loop(0, n_head, fill, 0)

    copy_o.wait()
    copy_g.wait()
    for h in range(n_head):
        prod = gv[:, h * D:(h + 1) * D].astype(F32) * ov[:, h * D:(h + 1) * D].astype(F32)
        sums = jnp.sum(prod.T, axis=0, keepdims=True)
        delta_out[h, :, :] = jnp.broadcast_to(sums, (8, ch))
    keep = pltpu.make_async_copy(delta_out.at[me], delta_in.at[me], d_rsem.at[me])
    keep.start()
    for by in (1, 3, 2):
        to = peer(by)
        send(delta_out.at[to], delta_in.at[me], d_ssem.at[by], d_rsem.at[me], (ctx, to))

    def got_own(a, j):
        arrived(chunk(a, 0, j), x_ssem.at[a, 0], x_rsem.at[a, j])

    def to_partner(a, row, slot, j):
        return remote(
            chunk(a, slot, j), chunk(a, 1, j), h_ssem.at[row, j], h_rsem.at[row, j], (partner, me)
        )

    def forward_rows(a, row, j):
        send(chunk(a, 0, j), chunk(a, 2, j), h_ssem.at[row, j], h_rsem.at[row, j], along(-2))

        @pl.when(odd == 1)
        def _():
            to_partner(a, row + 1, 0, j).start()

    def forward_cols(a, row, j):
        send(chunk(a, 0, j), chunk(a, 1, j), h_ssem.at[row, j], h_rsem.at[row, j], along(1))

    def relay(a, row, j):
        arrived(chunk(a, 2, j), h_ssem.at[row, j], h_rsem.at[row, j])

        @pl.when(odd == 0)
        def _():
            to_partner(a, row + 1, 2, j).start()

        sends.append(to_partner(a, row + 1, 0, j))

    def got_halo(a, row, slot, j):
        arrived(chunk(a, slot, j), h_ssem.at[row, j], h_rsem.at[row, j])

    order_in = (0, 1, 3, 2)

    def store_p(blk, tk, col, width):
        if blk == A:
            return p_ad.at[tk, :, pl.ds(col + ch, width)]
        if blk == DD:
            return p_ad.at[tk, :, pl.ds(col, width)]
        return (p_b if blk == B else p_c).at[tk, :, pl.ds(col, width)]

    def tile_1(blk, tk, col, masked):
        s = lax.dot_general(
            kx[KSLOT[blk], rows(tk), :], qx[QSLOT[blk], pl.ds(col, ch), :], NT_DIMS,
            preferred_element_type=F32,
        )
        if masked:
            apart = lax.broadcasted_iota(jnp.int32, (ch, ch), 1) - lax.broadcasted_iota(
                jnp.int32, (ch, ch), 0
            )
            seen = apart >= 0 if blk == A else apart < window - blk * n
            s = jnp.where(seen, s, -BIG)
        target = store_p(blk, tk, col, ch)
        for u in range(SUBS):
            part = s[u * sub:(u + 1) * sub] * TO_LOG2
            top = jnp.max(part, axis=0, keepdims=True)
            p = jnp.exp2(part - top)
            total = jnp.sum(p, axis=0, keepdims=True)
            target[u * sub:(u + 1) * sub, :] = p.astype(BF16)
            stat[blk * n_head + tk, u:u + 1, pl.ds(col, ch)] = top
            stat[blk * n_head + tk, SUBS + u:SUBS + u + 1, pl.ds(col, ch)] = total

    def phase_1(blk):
        if blk == A:
            for tk in range(n_head):
                for tq in range(tk, n_head):
                    tile_1(blk, tk, tq * ch, tq == tk)
        elif blk == DD:
            for tk in range(n_head):
                for tq in range(tk + 1):
                    tile_1(blk, tk, tq * ch, tq == tk)
        else:
            def body(tk, _):
                for u in range(n_head):
                    tq = lax.rem(tk + u, n_head)
                    tile_1(blk, tk, pl.multiple_of(tq * ch, ch), u == 0)
                return 0

            lax.fori_loop(0, n_head, body, 0)

    exists = (
        None,
        ctx + 1 < n_ctx,
        jnp.logical_and(ctx + 1 < n_ctx, ctx >= 1),
        jnp.logical_and(ctx + 2 < n_ctx, ctx >= 1),
    )
    tq_lane = lax.broadcasted_iota(jnp.int32, (1, n), 1) // ch

    def seen_row(blk, tk):
        if blk == A:
            return tq_lane >= tk
        upto = jnp.where(exists[blk], window - blk * n, -1)
        lower = jnp.logical_and(tq_lane <= tk, upto >= 0)
        upper = jnp.logical_and(tq_lane > tk, upto > 0)
        if blk == DD:
            return lower
        return jnp.logical_or(lower, upper)

    def shift(blk):
        return slope * (-blk * n * LOG2E)

    def tile_tops(blk, tk):
        tops = stat[blk * n_head + tk, 0:SUBS, :] + shift(blk)
        return jnp.where(seen_row(blk, tk), tops, -BIG)

    def combine(blks, tops, sums):
        top = tops
        for blk in blks:
            for tk in range(n_head):
                here = jnp.max(tile_tops(blk, tk), axis=0, keepdims=True)
                top = here if top is None else jnp.maximum(top, here)
        total = jnp.zeros((1, n), F32)
        for t, s in sums:
            total = total + s * jnp.exp2(t - top)
        for blk in blks:
            for tk in range(n_head):
                weight = jnp.exp2(tile_tops(blk, tk) - top)
                value = jnp.where(
                    seen_row(blk, tk), weight * stat[blk * n_head + tk, SUBS:2 * SUBS, :], 0.0
                )
                total = total + jnp.sum(value, axis=0, keepdims=True)
        return top, total

    def set_ratio(blk, lse):
        for tk in range(n_head):
            r = jnp.exp2(tile_tops(blk, tk) - lse)
            ratio[blk * n_head + tk, 0:SUBS, :] = jnp.where(seen_row(blk, tk), r, 0.0)

    def send_part(at, blks, by):
        top, total = combine(blks, None, ())
        part_out[at, 0:1, :] = top
        part_out[at, 1:2, :] = total
        send(part_out.at[at], part_in.at[at], s_ssem.at[at], s_rsem.at[at], along(by))

    def row_2(blk, tk, col, width, first_k, first_q, delta):
        qs, ks = QSLOT[blk], KSLOT[blk]
        cols = pl.ds(col, width)
        dp = lax.dot_general(
            vb[ks, rows(tk), :], gb[qs, cols, :], NT_DIMS, preferred_element_type=F32
        )
        delta_row = delta[:, cols]
        source = store_p(blk, tk, col, width)
        halves = []
        scores = []
        for u in range(SUBS):
            r = ratio[blk * n_head + tk, u:u + 1, cols].astype(BF16)
            half = source[u * sub:(u + 1) * sub, :] * r
            halves.append(half)
            scores.append(half * (dp[u * sub:(u + 1) * sub] - delta_row).astype(BF16))
        half = jnp.concatenate(halves, axis=0)
        score = jnp.concatenate(scores, axis=0)
        dv = jnp.dot(half, gb[qs, cols, :], preferred_element_type=F32)
        dk = jnp.dot(score, qx[qs, cols, 0:D], preferred_element_type=F32)
        dq = lax.dot_general(kx[ks, rows(tk), 0:D], score, TN_DIMS, preferred_element_type=F32)
        if first_k:
            dva[ks, rows(tk), :] = dv
            dka[ks, rows(tk), :] = dk
        else:
            dva[ks, rows(tk), :] += dv
            dka[ks, rows(tk), :] += dk
        if first_q:
            dqt[qs, :, cols] = dq
        else:
            dqt[qs, :, cols] += dq

    def send_dq(at, slot, by):
        for step in range(n_head):
            j = peer(step + 1)
            cols = pl.ds(pl.multiple_of(j * ch, ch), ch)
            dq_send[at, j, :, :] = dqt[slot, :, cols].astype(BF16)
            send(
                dq_send.at[at, j], dq_recv.at[at, j], dq_ssem.at[at, j], dq_rsem.at[at, j], along(by)
            )

    outs = (dq_out, dk_out, dv_out)

    def give(which, j):
        return remote(
            fin.at[which, j], outs[which].at[:, lanes(me)], o_ssem.at[which, j], o_rsem.at[which, me],
            (ctx, j),
        )

    def keep_out(which):
        return pltpu.make_async_copy(
            fin.at[which, me], outs[which].at[:, lanes(me)], o_rsem.at[which, me]
        )

    for by in order_in:
        j = peer(by)
        got_own(0, j)
        forward_rows(0, 0, j)
        got_own(1, j)
        forward_cols(1, 4, j)
    phase_1(A)
    for by in order_in:
        relay(0, 0, peer(by))
    for by in order_in:
        got_halo(1, 4, 1, peer(by))
    phase_1(DD)
    send_part(1, (DD,), 2)
    for by in order_in:
        j = peer(by)
        got_own(2, j)
        forward_rows(2, 2, j)
        got_own(3, j)
        forward_cols(3, 5, j)
    for by in order_in:
        got_halo(0, 1, 1, peer(by))
    phase_1(C)
    phase_1(B)
    send_part(0, (B, C), 1)
    for by in order_in:
        relay(2, 2, peer(by))
    for by in order_in:
        j = peer(by)
        arrived(delta_in.at[j], d_ssem.at[0], d_rsem.at[j])
    delta_own = jnp.concatenate([delta_in[j, 0:1, :] for j in range(n_head)], axis=1)
    for at in range(2):
        arrived(part_in.at[at], s_ssem.at[at], s_rsem.at[at])
    tops = [part_in[at, 0:1, :] for at in range(2)]
    sums = [(tops[at], part_in[at, 1:2, :]) for at in range(2)]
    top, total = combine((A,), jnp.maximum(tops[0], tops[1]), sums)
    lse = top + jnp.log(total) * LOG2E
    ret_out[0:1, :] = lse
    ret_out[1:2, :] = delta_own
    for at in range(2):
        send(ret_out, ret_in.at[at], s_ssem.at[2 + at], s_rsem.at[2 + at], along(-1 - at))
    set_ratio(A, lse)
    delta_a = ret_out.at[1:2, :]
    for tk in range(n_head):
        row_2(A, tk, tk * ch, n - tk * ch, True, tk == 0, delta_a)

    arrived(ret_in.at[1], s_ssem.at[3], s_rsem.at[3])
    set_ratio(DD, ret_in[1, 0:1, :])
    for by in order_in:
        got_halo(3, 5, 1, peer(by))
    delta_d = ret_in.at[1, 1:2, :]
    for tk in reversed(range(n_head)):
        row_2(DD, tk, 0, (tk + 1) * ch, True, tk == n_head - 1, delta_d)
    send_dq(1, 2, 2)

    arrived(ret_in.at[0], s_ssem.at[2], s_rsem.at[2])
    set_ratio(C, ret_in[0, 0:1, :])
    set_ratio(B, ret_in[0, 0:1, :])
    for by in order_in:
        got_halo(2, 3, 1, peer(by))
    delta_bc = ret_in.at[0, 1:2, :]
    dqt[1, :, :] = jnp.zeros((D, n), F32)

    def give_kv(which, j):
        return remote(
            dkv_send.at[which, j], dkv_recv.at[which, j], kv_ssem.at[which, j], kv_rsem.at[which, j],
            along(-1),
        )

    def step_c(step, _):
        tk = lax.rem(me + 1 + step, n_head)
        row_2(C, tk, 0, n, False, False, delta_bc)
        dkv_send[0, tk, :, :] = dka[1, rows(tk), :].astype(BF16)
        dkv_send[1, tk, :, :] = dva[1, rows(tk), :].astype(BF16)
        for which in range(2):
            give_kv(which, tk).start()
        return 0

    lax.fori_loop(0, n_head, step_c, 0)

    def step_b(step, _):
        tk = lax.rem(me + 1 + step, n_head)
        row_2(B, tk, 0, n, False, False, delta_bc)
        for which in range(2):
            give_kv(which, tk).wait_recv()
        dk = dka[0, rows(tk), :] + dkv_recv[0, tk, :, :].astype(F32)
        dv = dva[0, rows(tk), :] + dkv_recv[1, tk, :, :].astype(F32)
        fin[1, tk, :, :] = (dk * SCALE).astype(BF16)
        fin[2, tk, :, :] = dv.astype(BF16)

        @pl.when(step < n_head - 1)
        def _():
            give(1, tk).start()
            give(2, tk).start()

        return 0

    lax.fori_loop(0, n_head, step_b, 0)
    send_dq(0, 1, 1)
    keep_out(1).start()
    keep_out(2).start()
    for step in range(n_head):
        j = peer(step + 1)
        for at in (1, 0):
            arrived(dq_recv.at[at, j], dq_ssem.at[at, j], dq_rsem.at[at, j])
        cols = pl.ds(pl.multiple_of(j * ch, ch), ch)
        dq = dqt[0, :, cols] + dq_recv[0, j, :, :].astype(F32) + dq_recv[1, j, :, :].astype(F32)
        fin[0, j, :, :] = (dq.T * SCALE).astype(BF16)
        if step < n_head - 1:
            give(0, j).start()
    keep_out(0).start()

    for which in range(3):
        for step in range(n_head - 1):
            give(which, peer(step + 1)).wait_send()
    for which in range(2):
        for j in range(n_head):
            give_kv(which, j).wait_send()
    for copy in sends:
        copy.wait_send()
    for which in range(3):
        for step in range(n_head):
            j = peer(step)
            arrived(outs[which].at[:, lanes(j)], o_ssem.at[which, j], o_rsem.at[which, j])


def solution(mesh):
    n_ctx, n_head = mesh.shape["ctx"], mesh.shape["head"]

    def body(queries, keys, values, output, out_grad, slopes, windows):
        ch, width = queries.shape
        n = ch * n_head
        smem = pl.BlockSpec(memory_space=pltpu.SMEM)
        hbm = pl.BlockSpec(memory_space=pl.ANY)
        dma = pltpu.SemaphoreType.DMA
        vmem = pltpu.VMEM
        out = jax.ShapeDtypeStruct((ch, width), BF16)
        return pl.pallas_call(
            functools.partial(kernel, n_ctx, n_head),
            out_shape=[out] * 3,
            in_specs=[smem, smem] + [hbm] * 5,
            out_specs=[hbm] * 3,
            scratch_shapes=[
                vmem((3, n, 2 * D), BF16),
                vmem((2, n, 2 * D), BF16),
                vmem((3, n, D), BF16),
                vmem((2, n, D), BF16),
                vmem((ch, width), BF16),
                vmem((ch, width), BF16),
                vmem((n_head, ch, n + ch), BF16),
                vmem((n_head, ch, n), BF16),
                vmem((n_head, ch, n), BF16),
                vmem((4 * n_head, 2 * SUBS, n), F32),
                vmem((4 * n_head, SUBS, n), F32),
                vmem((3, D, n), F32),
                vmem((2, n, D), F32),
                vmem((2, n, D), F32),
                vmem((n_head, 8, ch), F32),
                vmem((n_head, 8, ch), F32),
                vmem((2, 8, n), F32),
                vmem((2, 8, n), F32),
                vmem((8, n), F32),
                vmem((2, 8, n), F32),
                vmem((2, n_head, D, ch), BF16),
                vmem((2, n_head, D, ch), BF16),
                vmem((2, n_head, ch, D), BF16),
                vmem((2, n_head, ch, D), BF16),
                vmem((3, n_head, ch, D), BF16),
                dma((4, n_head)),
                dma((4, n_head)),
                dma((6, n_head)),
                dma((6, n_head)),
                dma((n_head,)),
                dma((n_head,)),
                dma((4,)),
                dma((4,)),
                dma((2, n_head)),
                dma((2, n_head)),
                dma((2, n_head)),
                dma((2, n_head)),
                dma((3, n_head)),
                dma((3, n_head)),
                dma((2,)),
            ],
            compiler_params=pltpu.CompilerParams(
                collective_id=0, has_side_effects=True, vmem_limit_bytes=62 << 20
            ),
            cost_estimate=pl.CostEstimate(
                flops=2 * 5 * 3 * n * n * D, bytes_accessed=8 * ch * width * 2,
                transcendentals=3 * n * n,
            ),
        )(slopes, windows, queries, keys, values, output, out_grad)

    split = P(("ctx", "head"), None)
    return jax.shard_map(
        body,
        mesh=mesh,
        in_specs=(split,) * 5 + (P(), P()),
        out_specs=(split,) * 3,
        check_vma=False,
    )
```

```python
import functools
import math

import jax
import jax.numpy as jnp
from jax import lax
from jax.experimental import pallas as pl
from jax.experimental.pallas import tpu as pltpu
from jax.sharding import PartitionSpec as P

D = 128
SCALE = D ** (-0.5)
LOG2E = math.log2(math.e)
TO_LOG2 = SCALE * LOG2E
BIG = 1e30
F32 = jnp.float32
BF16 = jnp.bfloat16
MESH = pl.DeviceIdType.MESH
SUBS = 4
NT_DIMS = (((1,), (1,)), ((), ()))
TN_DIMS = (((0,), (0,)), ((), ()))

A, B, C, DD = range(4)
QSLOT = (0, 1, 1, 2)
KSLOT = (0, 0, 1, 1)


def kernel(
    n_ctx,
    n_head,
    slopes,
    windows,
    q_in,
    k_in,
    v_in,
    o_in,
    g_in,
    dq_out,
    dk_out,
    dv_out,
    qx,
    kx,
    gb,
    vb,
    ov,
    gv,
    p_ad,
    p_b,
    p_c,
    stat,
    ratio,
    dqt,
    dka,
    dva,
    delta_out,
    delta_in,
    part_out,
    part_in,
    ret_out,
    ret_in,
    deltas,
    dq_send,
    dq_recv,
    dkv_send,
    dkv_recv,
    fin,
    x_ssem,
    x_rsem,
    h_ssem,
    h_rsem,
    d_ssem,
    d_rsem,
    s_ssem,
    s_rsem,
    dq_ssem,
    dq_rsem,
    kv_ssem,
    kv_rsem,
    o_ssem,
    o_rsem,
    l_sem,
):
    ch = q_in.shape[0]
    n = n_head * ch
    sub = ch // SUBS
    ctx = lax.axis_index("ctx")
    me = lax.axis_index("head")
    odd = lax.rem(ctx, 2)
    partner = ctx + 1 - 2 * odd

    def along(by):
        return (lax.rem(ctx + by + n_ctx, n_ctx), me)

    def peer(by):
        return lax.rem(me + by, n_head)

    def rows(j):
        return pl.ds(pl.multiple_of(j * ch, ch), ch)

    def lanes(j):
        return pl.ds(pl.multiple_of(j * D, D), D)

    def remote(src, dst, ssem, rsem, device):
        return pltpu.make_async_remote_copy(
            src_ref=src, dst_ref=dst, send_sem=ssem, recv_sem=rsem,
            device_id=device, device_id_type=MESH,
        )

    sends = []

    def send(src, dst, ssem, rsem, device):
        copy = remote(src, dst, ssem, rsem, device)
        copy.start()
        sends.append(copy)

    def arrived(dst, ssem, rsem):
        remote(dst, dst, ssem, rsem, along(0)).wait_recv()

    slope = slopes[me]
    window = windows[me]

    bufs = (qx, kx, gb, vb)
    ins = (q_in, k_in, g_in, v_in)

    def chunk(a, slot, j):
        if a < 2:
            return bufs[a].at[slot, rows(j), 0:D]
        return bufs[a].at[slot, rows(j), :]

    own = []
    for a in range(4):
        copy = pltpu.make_async_copy(ins[a].at[:, lanes(me)], chunk(a, 0, me), x_rsem.at[a, me])
        copy.start()
        own.append(copy)
    copy_o = pltpu.make_async_copy(o_in, ov, l_sem.at[0])
    copy_g = pltpu.make_async_copy(g_in, gv, l_sem.at[1])
    copy_o.start()
    copy_g.start()

    barrier = pltpu.get_barrier_semaphore()
    neighbours = [along(1), along(-1), along(2), along(-2)]
    neighbours += [(ctx, peer(by)) for by in range(1, n_head)]
    for device in neighbours:
        pl.semaphore_signal(barrier, inc=1, device_id=device, device_id_type=MESH)
    pl.semaphore_wait(barrier, len(neighbours))

    first = ((0, 1), (0, 3), (1, 1), (1, 3), (0, 2), (1, 2))
    for a, by in first + ((2, 1), (2, 3), (2, 2), (3, 1), (3, 3), (3, 2)):
        to = peer(by)
        send(ins[a].at[:, lanes(to)], chunk(a, 0, me), x_ssem.at[a, by], x_rsem.at[a, me], (ctx, to))

    lane = lax.broadcasted_iota(jnp.int32, (1, D), 1)
    ones = jnp.broadcast_to(jnp.where(lane < 3, 1.0, 0.0), (ch, D)).astype(BF16)

    def fill(t, _):
        for slot in range(3):
            qx[slot, rows(t), D:] = ones
        pos = (lax.broadcasted_iota(jnp.int32, (ch, D), 0) + t * ch).astype(F32)
        bias = pos * (slope / SCALE)
        high = bias.astype(BF16).astype(F32)
        mid = (bias - high).astype(BF16).astype(F32)
        low = bias - high - mid
        terms = jnp.where(lane == 0, high, jnp.where(lane == 1, mid, jnp.where(lane == 2, low, 0.0)))
        for slot in range(2):
            kx[slot, rows(t), D:] = terms.astype(BF16)
        return 0

    lax.fori_loop(0, n_head, fill, 0)

    copy_o.wait()
    copy_g.wait()
    for h in range(n_head):
        prod = gv[:, h * D:(h + 1) * D].astype(F32) * ov[:, h * D:(h + 1) * D].astype(F32)
        sums = jnp.sum(prod.T, axis=0, keepdims=True)
        delta_out[h, :, :] = jnp.broadcast_to(sums, (8, ch))
    keep = pltpu.make_async_copy(delta_out.at[me], delta_in.at[me], d_rsem.at[me])
    keep.start()
    for by in (1, 3, 2):
        to = peer(by)
        send(delta_out.at[to], delta_in.at[me], d_ssem.at[by], d_rsem.at[me], (ctx, to))

    def got_own(a, j):
        arrived(chunk(a, 0, j), x_ssem.at[a, 0], x_rsem.at[a, j])

    def to_partner(a, row, slot, j):
        return remote(
            chunk(a, slot, j), chunk(a, 1, j), h_ssem.at[row, j], h_rsem.at[row, j], (partner, me)
        )

    def forward_rows(a, row, j):
        send(chunk(a, 0, j), chunk(a, 2, j), h_ssem.at[row, j], h_rsem.at[row, j], along(-2))

        @pl.when(odd == 1)
        def _():
            to_partner(a, row + 1, 0, j).start()

    def forward_cols(a, row, j):
        send(chunk(a, 0, j), chunk(a, 1, j), h_ssem.at[row, j], h_rsem.at[row, j], along(1))

    def relay(a, row, j):
        arrived(chunk(a, 2, j), h_ssem.at[row, j], h_rsem.at[row, j])

        @pl.when(odd == 0)
        def _():
            to_partner(a, row + 1, 2, j).start()

        sends.append(to_partner(a, row + 1, 0, j))

    def got_halo(a, row, slot, j):
        arrived(chunk(a, slot, j), h_ssem.at[row, j], h_rsem.at[row, j])

    order_in = (0, 1, 3, 2)

    def store_p(blk, tk, col, width):
        if blk == A:
            return p_ad.at[tk, :, pl.ds(col + ch, width)]
        if blk == DD:
            return p_ad.at[tk, :, pl.ds(col, width)]
        return (p_b if blk == B else p_c).at[tk, :, pl.ds(col, width)]

    def tile_1(blk, tk, col, masked):
        s = lax.dot_general(
            kx[KSLOT[blk], rows(tk), :], qx[QSLOT[blk], pl.ds(col, ch), :], NT_DIMS,
            preferred_element_type=F32,
        )
        target = store_p(blk, tk, col, ch)
        for u in range(SUBS):
            part = s[u * sub:(u + 1) * sub]
            if masked:
                apart = lax.broadcasted_iota(jnp.int32, (sub, sub), 1) - lax.broadcasted_iota(
                    jnp.int32, (sub, sub), 0
                )
                seen = apart >= 0 if blk == A else apart < window - blk * n
                pieces = [jnp.where(seen, part[:, u * sub:(u + 1) * sub], -BIG)]
                if u > 0:
                    pieces.insert(0, part[:, :u * sub])
                if u < SUBS - 1:
                    pieces.append(part[:, (u + 1) * sub:])
                part = jnp.concatenate(pieces, axis=1)
            top = jnp.max(part, axis=0, keepdims=True)
            p = jnp.exp2((part - top) * TO_LOG2)
            total = jnp.sum(p, axis=0, keepdims=True)
            target[u * sub:(u + 1) * sub, :] = p.astype(BF16)
            stat[blk * n_head + tk, u:u + 1, pl.ds(col, ch)] = top * TO_LOG2
            stat[blk * n_head + tk, SUBS + u:SUBS + u + 1, pl.ds(col, ch)] = total

    half_n = n // 2
    half_c = n_head // 2
    halves_of = [pl.ds(h * half_n, half_n) for h in range(2)]

    def phase_1(blk, h):
        for tk in range(n_head):
            for tq in range(h * half_c, (h + 1) * half_c):
                if blk != DD or tq <= tk:
                    tile_1(blk, tk, tq * ch, tq == tk)

    exists = (
        None,
        ctx + 1 < n_ctx,
        jnp.logical_and(ctx + 1 < n_ctx, ctx >= 1),
        jnp.logical_and(ctx + 2 < n_ctx, ctx >= 1),
    )
    q_part = lax.broadcasted_iota(jnp.int32, (SUBS, half_n), 1) // sub
    k_part = lax.broadcasted_iota(jnp.int32, (SUBS, half_n), 0)

    def seen_row(blk, tk, h):
        apart = q_part + h * half_c * SUBS - (k_part + tk * SUBS)
        if blk == A:
            return apart >= 0
        upto = jnp.where(exists[blk], window - blk * n, -1)
        return jnp.where(apart <= 0, upto, upto - 1) >= 0

    def shift(blk):
        return slope * (-blk * n * LOG2E)

    def tile_tops(blk, tk, h):
        tops = stat[blk * n_head + tk, 0:SUBS, halves_of[h]] + shift(blk)
        return jnp.where(seen_row(blk, tk, h), tops, -BIG)

    def tiles_in(blk, h):
        if blk == A:
            return range((h + 1) * half_c)
        if blk == DD:
            return range(h * half_c, n_head)
        return range(n_head)

    def combine(blks, h, parts):
        tops = [tile_tops(blk, tk, h) for blk in blks for tk in tiles_in(blk, h)]
        tall = functools.reduce(jnp.maximum, tops)
        top = jnp.max(tall, axis=0, keepdims=True)
        for t, _ in parts:
            top = jnp.maximum(top, t)
        total = jnp.zeros((1, half_n), F32)
        for t, v in parts:
            total = total + v * jnp.exp2(t - top)
        several = jnp.zeros((SUBS, half_n), F32)
        i = 0
        for blk in blks:
            for tk in tiles_in(blk, h):
                sums = stat[blk * n_head + tk, SUBS:2 * SUBS, halves_of[h]]
                several = several + jnp.where(
                    seen_row(blk, tk, h), jnp.exp2(tops[i] - top) * sums, 0.0
                )
                i += 1
        return top, total + jnp.sum(several, axis=0, keepdims=True)

    def set_ratio(blk, h, lse):
        for tk in tiles_in(blk, h):
            r = jnp.exp2(tile_tops(blk, tk, h) - lse)
            ratio[blk * n_head + tk, 0:SUBS, halves_of[h]] = jnp.where(seen_row(blk, tk, h), r, 0.0)

    def send_part(at, h, blks):
        top, total = combine(blks, h, ())
        part_out[at, h, 0:1, :] = top
        part_out[at, h, 1:2, :] = total
        i = at * 2 + h
        send(part_out.at[at, h], part_in.at[at, h], s_ssem.at[i], s_rsem.at[i], along(1 + at))

    def send_lse(h):
        for at in range(2):
            i = at * 2 + h
            arrived(part_in.at[at, h], s_ssem.at[i], s_rsem.at[i])
        parts = [(part_in[at, h, 0:1, :], part_in[at, h, 1:2, :]) for at in range(2)]
        top, total = combine((A,), h, parts)
        lse = top + jnp.log(total) * LOG2E
        ret_out[h, 0:1, :] = lse
        ret_out[h, 1:2, :] = deltas[0:1, halves_of[h]]
        for at in (1, 0):
            i = 4 + at * 2 + h
            send(ret_out.at[h], ret_in.at[at, h], s_ssem.at[i], s_rsem.at[i], along(-1 - at))
        set_ratio(A, h, lse)

    def got_lse(at, h, blks):
        i = 4 + at * 2 + h
        arrived(ret_in.at[at, h], s_ssem.at[i], s_rsem.at[i])
        deltas[1 + at:2 + at, halves_of[h]] = ret_in[at, h, 1:2, :]
        for blk in blks:
            set_ratio(blk, h, ret_in[at, h, 0:1, :])

    def row_2(blk, tk, col, width, first_k, first_q):
        qs, ks = QSLOT[blk], KSLOT[blk]
        cols = pl.ds(col, width)
        dp = lax.dot_general(
            vb[ks, rows(tk), :], gb[qs, cols, :], NT_DIMS, preferred_element_type=F32
        )
        delta_row = deltas[qs:qs + 1, cols]
        source = store_p(blk, tk, col, width)
        halves = []
        scores = []
        for u in range(SUBS):
            r = ratio[blk * n_head + tk, u:u + 1, cols].astype(BF16)
            half = source[u * sub:(u + 1) * sub, :] * r
            halves.append(half)
            scores.append(half * (dp[u * sub:(u + 1) * sub] - delta_row).astype(BF16))
        half = jnp.concatenate(halves, axis=0)
        score = jnp.concatenate(scores, axis=0)
        dv = jnp.dot(half, gb[qs, cols, :], preferred_element_type=F32)
        dk = jnp.dot(score, qx[qs, cols, 0:D], preferred_element_type=F32)
        dq = lax.dot_general(kx[ks, rows(tk), 0:D], score, TN_DIMS, preferred_element_type=F32)
        if first_k:
            dva[ks, rows(tk), :] = dv
            dka[ks, rows(tk), :] = dk
        else:
            dva[ks, rows(tk), :] += dv
            dka[ks, rows(tk), :] += dk
        if first_q:
            dqt[qs, :, cols] = dq
        else:
            dqt[qs, :, cols] += dq

    def send_dq(at, slot, by):
        for step in range(n_head):
            j = peer(step + 1)
            cols = pl.ds(pl.multiple_of(j * ch, ch), ch)
            dq_send[at, j, :, :] = dqt[slot, :, cols].astype(BF16)
            send(
                dq_send.at[at, j], dq_recv.at[at, j], dq_ssem.at[at, j], dq_rsem.at[at, j], along(by)
            )

    outs = (dq_out, dk_out, dv_out)

    def give(which, j):
        return remote(
            fin.at[which, j], outs[which].at[:, lanes(me)], o_ssem.at[which, j], o_rsem.at[which, me],
            (ctx, j),
        )

    def keep_out(which):
        return pltpu.make_async_copy(
            fin.at[which, me], outs[which].at[:, lanes(me)], o_rsem.at[which, me]
        )

    near = [peer(by) for by in range(n_head)]

    def rows_on(a, row, bys):
        for by in bys:
            got_own(a, near[by])
            forward_rows(a, row, near[by])

    def cols_on(a, row, bys):
        for by in bys:
            got_own(a, near[by])
            forward_cols(a, row, near[by])

    here = []

    def tiles_of(by):
        j = near[by]
        tile_1(A, j, pl.multiple_of(j * ch, ch), True)
        for other in here:
            tk, tq = jnp.minimum(other, j), jnp.maximum(other, j)
            tile_1(A, tk, pl.multiple_of(tq * ch, ch), False)
        here.append(j)

    rows_on(0, 0, (0,))
    cols_on(1, 4, (0,))
    tiles_of(0)
    rows_on(0, 0, (1, 3))
    cols_on(1, 4, (1, 3))
    tiles_of(1)
    tiles_of(3)
    rows_on(0, 0, (2,))
    cols_on(1, 4, (2,))
    rows_on(2, 2, (0,))
    cols_on(3, 5, (0,))
    tiles_of(2)
    for by in order_in:
        relay(0, 0, near[by])
    for by in order_in:
        got_halo(1, 4, 1, near[by])
    phase_1(DD, 0)
    rows_on(2, 2, (1, 3))
    for by in order_in:
        got_halo(0, 1, 1, near[by])
    phase_1(C, 0)
    rows_on(2, 2, (2,))
    send_part(1, 0, (DD,))
    phase_1(B, 0)
    send_part(0, 0, (B, C))
    cols_on(3, 5, (1, 3))
    phase_1(DD, 1)
    send_part(1, 1, (DD,))
    phase_1(C, 1)
    cols_on(3, 5, (2,))
    for j in near:
        arrived(delta_in.at[j], d_ssem.at[0], d_rsem.at[j])
    deltas[0:1, :] = jnp.concatenate([delta_in[j, 0:1, :] for j in range(n_head)], axis=1)
    send_lse(0)
    phase_1(B, 1)
    send_part(0, 1, (B, C))
    for by in order_in:
        relay(2, 2, near[by])
    for slot in range(2):
        dqt[slot, :, :] = jnp.zeros((D, n), F32)

    got_lse(1, 0, (DD,))
    for by in order_in:
        got_halo(3, 5, 1, near[by])
    for tk in reversed(range(n_head)):
        row_2(DD, tk, 0, min(tk + 1, half_c) * ch, True, tk == n_head - 1)
    send_lse(1)
    got_lse(0, 0, (B, C))
    for by in order_in:
        got_halo(2, 3, 1, near[by])

    def first_c(tk, _):
        row_2(C, tk, 0, half_n, False, False)
        return 0

    lax.fori_loop(0, n_head, first_c, 0)
    got_lse(1, 1, (DD,))
    for tk in reversed(range(half_c, n_head)):
        row_2(DD, tk, half_n, (tk + 1 - half_c) * ch, False, tk == n_head - 1)
    send_dq(1, 2, 2)
    got_lse(0, 1, (B, C))

    def give_kv(which, j):
        return remote(
            dkv_send.at[which, j], dkv_recv.at[which, j], kv_ssem.at[which, j], kv_rsem.at[which, j],
            along(-1),
        )

    def give_dq(at, j, by):
        return remote(
            dq_send.at[at, j], dq_recv.at[at, j], dq_ssem.at[at, j], dq_rsem.at[at, j], along(by)
        )

    def step_c(step, _):
        tk = lax.rem(me + 1 + step, n_head)
        row_2(C, tk, half_n, half_n, False, False)
        dkv_send[0, tk, :, :] = dka[1, rows(tk), :].astype(BF16)
        dkv_send[1, tk, :, :] = dva[1, rows(tk), :].astype(BF16)
        for which in range(2):
            give_kv(which, tk).start()
        return 0

    lax.fori_loop(0, n_head, step_c, 0)

    def step_ab(step, _):
        tk = lax.rem(me + 1 + step, n_head)
        for at in range(n_head):

            @pl.when(tk == at)
            def _():
                row_2(A, at, at * ch, n - at * ch, True, False)

        @pl.when(step < n_head - 1)
        def _():
            row_2(B, tk, 0, n, False, False)

        @pl.when(step == n_head - 1)
        def _():
            def tile(i, _):
                tq = lax.rem(me + 1 + i, n_head)
                cols = pl.ds(pl.multiple_of(tq * ch, ch), ch)
                row_2(B, tk, pl.multiple_of(tq * ch, ch), ch, False, False)
                dq_send[0, tq, :, :] = dqt[1, :, cols].astype(BF16)
                give_dq(0, tq, 1).start()
                return 0

            lax.fori_loop(0, n_head, tile, 0)

        for which in range(2):
            give_kv(which, tk).wait_recv()
        dk = dka[0, rows(tk), :] + dkv_recv[0, tk, :, :].astype(F32)
        dv = dva[0, rows(tk), :] + dkv_recv[1, tk, :, :].astype(F32)
        fin[1, tk, :, :] = (dk * SCALE).astype(BF16)
        fin[2, tk, :, :] = dv.astype(BF16)

        @pl.when(step < n_head - 1)
        def _():
            give(1, tk).start()
            give(2, tk).start()

        return 0

    lax.fori_loop(0, n_head, step_ab, 0)
    keep_out(1).start()
    keep_out(2).start()
    for step in range(n_head):
        j = peer(step + 1)
        for at in (1, 0):
            arrived(dq_recv.at[at, j], dq_ssem.at[at, j], dq_rsem.at[at, j])
        cols = pl.ds(pl.multiple_of(j * ch, ch), ch)
        dq = dqt[0, :, cols] + dq_recv[0, j, :, :].astype(F32) + dq_recv[1, j, :, :].astype(F32)
        fin[0, j, :, :] = (dq.T * SCALE).astype(BF16)
        if step < n_head - 1:
            give(0, j).start()
    keep_out(0).start()

    for j in range(n_head):
        give_dq(0, j, 1).wait_send()
    for which in range(3):
        for step in range(n_head - 1):
            give(which, peer(step + 1)).wait_send()
    for which in range(2):
        for j in range(n_head):
            give_kv(which, j).wait_send()
    for copy in sends:
        copy.wait_send()
    for which in range(3):
        for step in range(n_head):
            j = peer(step)
            arrived(outs[which].at[:, lanes(j)], o_ssem.at[which, j], o_rsem.at[which, j])


def copy_out(*refs):
    ins, outs, buf, sems = refs[:3], refs[3:6], refs[6], refs[7]
    parts = sems.shape[2]
    step = ins[0].shape[0] // parts
    moves = []
    for i in range(3):
        for j in range(parts):
            at = pl.ds(j * step, step)
            moves.append((
                pltpu.make_async_copy(ins[i].at[at], buf.at[i, at], sems.at[0, i, j]),
                pltpu.make_async_copy(buf.at[i, at], outs[i].at[at], sems.at[1, i, j]),
            ))
    for load, _ in moves:
        load.start()
    for load, store in moves:
        load.wait()
        store.start()
    for _, store in moves:
        store.wait()


def solution(mesh):
    n_ctx, n_head = mesh.shape["ctx"], mesh.shape["head"]

    def body(queries, keys, values, output, out_grad, slopes, windows):
        ch, width = queries.shape
        n = ch * n_head
        smem = pl.BlockSpec(memory_space=pltpu.SMEM)
        hbm = pl.BlockSpec(memory_space=pl.ANY)
        dma = pltpu.SemaphoreType.DMA
        vmem = pltpu.VMEM
        out = jax.ShapeDtypeStruct((ch, width), BF16)
        grads = pl.pallas_call(
            functools.partial(kernel, n_ctx, n_head),
            out_shape=[out] * 3,
            in_specs=[smem, smem] + [hbm] * 5,
            out_specs=[hbm] * 3,
            scratch_shapes=[
                vmem((3, n, 2 * D), BF16),
                vmem((2, n, 2 * D), BF16),
                vmem((3, n, D), BF16),
                vmem((2, n, D), BF16),
                vmem((ch, width), BF16),
                vmem((ch, width), BF16),
                vmem((n_head, ch, n + ch), BF16),
                vmem((n_head, ch, n), BF16),
                vmem((n_head, ch, n), BF16),
                vmem((4 * n_head, 2 * SUBS, n), F32),
                vmem((4 * n_head, SUBS, n), F32),
                vmem((3, D, n), F32),
                vmem((2, n, D), F32),
                vmem((2, n, D), F32),
                vmem((n_head, 8, ch), F32),
                vmem((n_head, 8, ch), F32),
                vmem((2, 2, 2, n // 2), F32),
                vmem((2, 2, 2, n // 2), F32),
                vmem((2, 2, n // 2), F32),
                vmem((2, 2, 2, n // 2), F32),
                vmem((3, n), F32),
                vmem((2, n_head, D, ch), BF16),
                vmem((2, n_head, D, ch), BF16),
                vmem((2, n_head, ch, D), BF16),
                vmem((2, n_head, ch, D), BF16),
                vmem((3, n_head, ch, D), BF16),
                dma((4, n_head)),
                dma((4, n_head)),
                dma((6, n_head)),
                dma((6, n_head)),
                dma((n_head,)),
                dma((n_head,)),
                dma((8,)),
                dma((8,)),
                dma((2, n_head)),
                dma((2, n_head)),
                dma((2, n_head)),
                dma((2, n_head)),
                dma((3, n_head)),
                dma((3, n_head)),
                dma((2,)),
            ],
            compiler_params=pltpu.CompilerParams(
                collective_id=0, has_side_effects=True, vmem_limit_bytes=62 << 20
            ),
            cost_estimate=pl.CostEstimate(
                flops=2 * 5 * 3 * n * n * D, bytes_accessed=8 * ch * width * 2,
                transcendentals=3 * n * n,
            ),
        )(slopes, windows, queries, keys, values, output, out_grad)
        return pl.pallas_call(
            copy_out,
            out_shape=[out] * 3,
            in_specs=[hbm] * 3,
            out_specs=[hbm] * 3,
            scratch_shapes=[vmem((3, ch, width), BF16), dma((2, 3, 2))],
        )(*grads)

    split = P(("ctx", "head"), None)
    return jax.shard_map(
        body,
        mesh=mesh,
        in_specs=(split,) * 5 + (P(), P()),
        out_specs=(split,) * 3,
        check_vma=False,
    )
```

```python
import functools
import math

import jax
import jax.numpy as jnp
from jax import lax
from jax.experimental import pallas as pl
from jax.experimental.pallas import tpu as pltpu
from jax.sharding import PartitionSpec as P

D = 128
SCALE = D ** (-0.5)
LOG2E = math.log2(math.e)
TO_LOG2 = SCALE * LOG2E
BIG = 1e30
F32 = jnp.float32
BF16 = jnp.bfloat16
MESH = pl.DeviceIdType.MESH
SUBS = 4
NT_DIMS = (((1,), (1,)), ((), ()))
TN_DIMS = (((0,), (0,)), ((), ()))

A, B, C, DD = range(4)
QSLOT = (0, 1, 1, 2)
KSLOT = (0, 0, 1, 1)


def kernel(
    n_ctx,
    n_head,
    slopes,
    windows,
    q_in,
    k_in,
    v_in,
    o_in,
    g_in,
    dq_out,
    dk_out,
    dv_out,
    qx,
    kx,
    gb,
    vb,
    ov,
    gv,
    p_ad,
    p_b,
    p_c,
    stat,
    ratio,
    dqt,
    dka,
    dva,
    delta_out,
    delta_in,
    part_out,
    part_in,
    ret_out,
    ret_in,
    deltas,
    dq_send,
    dq_recv,
    dkv_send,
    dkv_recv,
    fin,
    x_ssem,
    x_rsem,
    h_ssem,
    h_rsem,
    d_ssem,
    d_rsem,
    s_ssem,
    s_rsem,
    dq_ssem,
    dq_rsem,
    kv_ssem,
    kv_rsem,
    o_ssem,
    o_rsem,
    l_sem,
):
    ch = q_in.shape[0]
    n = n_head * ch
    sub = ch // SUBS
    ctx = lax.axis_index("ctx")
    me = lax.axis_index("head")
    odd = lax.rem(ctx, 2)
    partner = ctx + 1 - 2 * odd

    def along(by):
        return (lax.rem(ctx + by + n_ctx, n_ctx), me)

    def peer(by):
        return lax.rem(me + by, n_head)

    def rows(j):
        return pl.ds(pl.multiple_of(j * ch, ch), ch)

    def lanes(j):
        return pl.ds(pl.multiple_of(j * D, D), D)

    def remote(src, dst, ssem, rsem, device):
        return pltpu.make_async_remote_copy(
            src_ref=src, dst_ref=dst, send_sem=ssem, recv_sem=rsem,
            device_id=device, device_id_type=MESH,
        )

    sends = []

    def send(src, dst, ssem, rsem, device):
        copy = remote(src, dst, ssem, rsem, device)
        copy.start()
        sends.append(copy)

    def arrived(dst, ssem, rsem):
        remote(dst, dst, ssem, rsem, along(0)).wait_recv()

    slope = slopes[me]
    window = windows[me]

    bufs = (qx, kx, gb, vb)
    ins = (q_in, k_in, g_in, v_in)

    def chunk(a, slot, j):
        if a < 2:
            return bufs[a].at[slot, rows(j), 0:D]
        return bufs[a].at[slot, rows(j), :]

    own = []
    for a in range(4):
        copy = pltpu.make_async_copy(ins[a].at[:, lanes(me)], chunk(a, 0, me), x_rsem.at[a, me])
        copy.start()
        own.append(copy)
    copy_o = pltpu.make_async_copy(o_in, ov, l_sem.at[0])
    copy_g = pltpu.make_async_copy(g_in, gv, l_sem.at[1])
    copy_o.start()
    copy_g.start()

    barrier = pltpu.get_barrier_semaphore()
    neighbours = [along(1), along(-1), along(2), along(-2)]
    neighbours += [(ctx, peer(by)) for by in range(1, n_head)]
    for device in neighbours:
        pl.semaphore_signal(barrier, inc=1, device_id=device, device_id_type=MESH)
    pl.semaphore_wait(barrier, len(neighbours))

    first = ((0, 1), (0, 3), (1, 1), (1, 3), (0, 2), (1, 2))
    for a, by in first + ((2, 1), (2, 3), (2, 2), (3, 1), (3, 3), (3, 2)):
        to = peer(by)
        send(ins[a].at[:, lanes(to)], chunk(a, 0, me), x_ssem.at[a, by], x_rsem.at[a, me], (ctx, to))

    lane = lax.broadcasted_iota(jnp.int32, (1, D), 1)
    ones = jnp.broadcast_to(jnp.where(lane < 3, 1.0, 0.0), (ch, D)).astype(BF16)

    def fill(t, _):
        for slot in range(3):
            qx[slot, rows(t), D:] = ones
        pos = (lax.broadcasted_iota(jnp.int32, (ch, D), 0) + t * ch).astype(F32)
        bias = pos * (slope / SCALE)
        high = bias.astype(BF16).astype(F32)
        mid = (bias - high).astype(BF16).astype(F32)
        low = bias - high - mid
        terms = jnp.where(lane == 0, high, jnp.where(lane == 1, mid, jnp.where(lane == 2, low, 0.0)))
        for slot in range(2):
            kx[slot, rows(t), D:] = terms.astype(BF16)
        return 0

    lax.fori_loop(0, n_head, fill, 0)

    for slot in range(2):
        dqt[slot, :, :] = jnp.zeros((D, n), F32)

    copy_o.wait()
    copy_g.wait()
    for h in range(n_head):
        prod = gv[:, h * D:(h + 1) * D].astype(F32) * ov[:, h * D:(h + 1) * D].astype(F32)
        sums = jnp.sum(prod.T, axis=0, keepdims=True)
        delta_out[h, :, :] = jnp.broadcast_to(sums, (8, ch))
    keep = pltpu.make_async_copy(delta_out.at[me], delta_in.at[me], d_rsem.at[me])
    keep.start()
    for by in (1, 3, 2):
        to = peer(by)
        send(delta_out.at[to], delta_in.at[me], d_ssem.at[by], d_rsem.at[me], (ctx, to))

    def got_own(a, j):
        arrived(chunk(a, 0, j), x_ssem.at[a, 0], x_rsem.at[a, j])

    def to_partner(a, row, slot, j):
        return remote(
            chunk(a, slot, j), chunk(a, 1, j), h_ssem.at[row, j], h_rsem.at[row, j], (partner, me)
        )

    def forward_rows(a, row, j):
        send(chunk(a, 0, j), chunk(a, 2, j), h_ssem.at[row, j], h_rsem.at[row, j], along(-2))

        @pl.when(odd == 1)
        def _():
            to_partner(a, row + 1, 0, j).start()

    def forward_cols(a, row, j):
        send(chunk(a, 0, j), chunk(a, 1, j), h_ssem.at[row, j], h_rsem.at[row, j], along(1))

    def relay(a, row, j):
        arrived(chunk(a, 2, j), h_ssem.at[row, j], h_rsem.at[row, j])

        @pl.when(odd == 0)
        def _():
            to_partner(a, row + 1, 2, j).start()

        sends.append(to_partner(a, row + 1, 0, j))

    def got_halo(a, row, slot, j):
        arrived(chunk(a, slot, j), h_ssem.at[row, j], h_rsem.at[row, j])

    order_in = (0, 1, 3, 2)

    def store_p(blk, tk, col, width):
        if blk == A:
            return p_ad.at[tk, :, pl.ds(col + ch, width)]
        if blk == DD:
            return p_ad.at[tk, :, pl.ds(col, width)]
        return (p_b if blk == B else p_c).at[tk, :, pl.ds(col, width)]

    def tile_1(blk, tk, col, masked):
        s = lax.dot_general(
            kx[KSLOT[blk], rows(tk), :], qx[QSLOT[blk], pl.ds(col, ch), :], NT_DIMS,
            preferred_element_type=F32,
        )
        target = store_p(blk, tk, col, ch)
        for u in range(SUBS):
            part = s[u * sub:(u + 1) * sub]
            if masked:
                apart = lax.broadcasted_iota(jnp.int32, (sub, sub), 1) - lax.broadcasted_iota(
                    jnp.int32, (sub, sub), 0
                )
                seen = apart >= 0 if blk == A else apart < window - blk * n
                pieces = [jnp.where(seen, part[:, u * sub:(u + 1) * sub], -BIG)]
                if u > 0:
                    pieces.insert(0, part[:, :u * sub])
                if u < SUBS - 1:
                    pieces.append(part[:, (u + 1) * sub:])
                part = jnp.concatenate(pieces, axis=1)
            top = jnp.max(part, axis=0, keepdims=True)
            p = jnp.exp2((part - top) * TO_LOG2)
            total = jnp.sum(p, axis=0, keepdims=True)
            target[u * sub:(u + 1) * sub, :] = p.astype(BF16)
            stat[blk * n_head + tk, u:u + 1, pl.ds(col, ch)] = top * TO_LOG2
            stat[blk * n_head + tk, SUBS + u:SUBS + u + 1, pl.ds(col, ch)] = total

    half_n = n // 2
    half_c = n_head // 2
    halves_of = [pl.ds(h * half_n, half_n) for h in range(2)]

    def phase_1(blk, h):
        for tk in range(n_head):
            for tq in range(h * half_c, (h + 1) * half_c):
                if blk != DD or tq <= tk:
                    tile_1(blk, tk, tq * ch, tq == tk)

    exists = (
        None,
        ctx + 1 < n_ctx,
        jnp.logical_and(ctx + 1 < n_ctx, ctx >= 1),
        jnp.logical_and(ctx + 2 < n_ctx, ctx >= 1),
    )
    q_part = lax.broadcasted_iota(jnp.int32, (SUBS, half_n), 1) // sub
    k_part = lax.broadcasted_iota(jnp.int32, (SUBS, half_n), 0)

    def seen_row(blk, tk, h):
        apart = q_part + h * half_c * SUBS - (k_part + tk * SUBS)
        if blk == A:
            return apart >= 0
        upto = jnp.where(exists[blk], window - blk * n, -1)
        return jnp.where(apart <= 0, upto, upto - 1) >= 0

    def shift(blk):
        return slope * (-blk * n * LOG2E)

    def tile_tops(blk, tk, h):
        tops = stat[blk * n_head + tk, 0:SUBS, halves_of[h]] + shift(blk)
        return jnp.where(seen_row(blk, tk, h), tops, -BIG)

    def tiles_in(blk, h):
        if blk == A:
            return range((h + 1) * half_c)
        if blk == DD:
            return range(h * half_c, n_head)
        return range(n_head)

    def combine(blks, h, parts):
        tops = [tile_tops(blk, tk, h) for blk in blks for tk in tiles_in(blk, h)]
        tall = functools.reduce(jnp.maximum, tops)
        top = jnp.max(tall, axis=0, keepdims=True)
        for t, _ in parts:
            top = jnp.maximum(top, t)
        total = jnp.zeros((1, half_n), F32)
        for t, v in parts:
            total = total + v * jnp.exp2(t - top)
        several = jnp.zeros((SUBS, half_n), F32)
        i = 0
        for blk in blks:
            for tk in tiles_in(blk, h):
                sums = stat[blk * n_head + tk, SUBS:2 * SUBS, halves_of[h]]
                several = several + jnp.where(
                    seen_row(blk, tk, h), jnp.exp2(tops[i] - top) * sums, 0.0
                )
                i += 1
        return top, total + jnp.sum(several, axis=0, keepdims=True)

    def set_ratio(blk, h, lse):
        for tk in tiles_in(blk, h):
            r = jnp.exp2(tile_tops(blk, tk, h) - lse)
            ratio[blk * n_head + tk, 0:SUBS, halves_of[h]] = jnp.where(seen_row(blk, tk, h), r, 0.0)

    def send_part(at, h, blks):
        top, total = combine(blks, h, ())
        part_out[at, h, 0:1, :] = top
        part_out[at, h, 1:2, :] = total
        i = at * 2 + h
        send(part_out.at[at, h], part_in.at[at, h], s_ssem.at[i], s_rsem.at[i], along(1 + at))

    def send_lse(h):
        for at in range(2):
            i = at * 2 + h
            arrived(part_in.at[at, h], s_ssem.at[i], s_rsem.at[i])
        parts = [(part_in[at, h, 0:1, :], part_in[at, h, 1:2, :]) for at in range(2)]
        top, total = combine((A,), h, parts)
        lse = top + jnp.log(total) * LOG2E
        ret_out[h, 0:1, :] = lse
        ret_out[h, 1:2, :] = deltas[0:1, halves_of[h]]
        for at in (1, 0):
            i = 4 + at * 2 + h
            send(ret_out.at[h], ret_in.at[at, h], s_ssem.at[i], s_rsem.at[i], along(-1 - at))
        set_ratio(A, h, lse)

    def got_lse(at, h, blks):
        i = 4 + at * 2 + h
        arrived(ret_in.at[at, h], s_ssem.at[i], s_rsem.at[i])
        deltas[1 + at:2 + at, halves_of[h]] = ret_in[at, h, 1:2, :]
        for blk in blks:
            set_ratio(blk, h, ret_in[at, h, 0:1, :])

    def row_2(blk, tk, col, width, first_k, first_q):
        qs, ks = QSLOT[blk], KSLOT[blk]
        cols = pl.ds(col, width)
        dp = lax.dot_general(
            vb[ks, rows(tk), :], gb[qs, cols, :], NT_DIMS, preferred_element_type=F32
        )
        delta_row = deltas[qs:qs + 1, cols]
        source = store_p(blk, tk, col, width)
        halves = []
        scores = []
        for u in range(SUBS):
            r = ratio[blk * n_head + tk, u:u + 1, cols].astype(BF16)
            half = source[u * sub:(u + 1) * sub, :] * r
            halves.append(half)
            scores.append(half * (dp[u * sub:(u + 1) * sub] - delta_row).astype(BF16))
        half = jnp.concatenate(halves, axis=0)
        score = jnp.concatenate(scores, axis=0)
        dv = jnp.dot(half, gb[qs, cols, :], preferred_element_type=F32)
        dk = jnp.dot(score, qx[qs, cols, 0:D], preferred_element_type=F32)
        dq = lax.dot_general(kx[ks, rows(tk), 0:D], score, TN_DIMS, preferred_element_type=F32)
        if first_k:
            dva[ks, rows(tk), :] = dv
            dka[ks, rows(tk), :] = dk
        else:
            dva[ks, rows(tk), :] += dv
            dka[ks, rows(tk), :] += dk
        if first_q:
            dqt[qs, :, cols] = dq
        else:
            dqt[qs, :, cols] += dq

    def send_dq(at, slot, by):
        for step in range(n_head):
            j = peer(step + 1)
            cols = pl.ds(pl.multiple_of(j * ch, ch), ch)
            dq_send[at, j, :, :] = dqt[slot, :, cols].astype(BF16)
            send(
                dq_send.at[at, j], dq_recv.at[at, j], dq_ssem.at[at, j], dq_rsem.at[at, j], along(by)
            )

    outs = (dq_out, dk_out, dv_out)

    def give(which, j):
        return remote(
            fin.at[which, j], outs[which].at[:, lanes(me)], o_ssem.at[which, j], o_rsem.at[which, me],
            (ctx, j),
        )

    def keep_out(which):
        return pltpu.make_async_copy(
            fin.at[which, me], outs[which].at[:, lanes(me)], o_rsem.at[which, me]
        )

    near = [peer(by) for by in range(n_head)]

    def rows_on(a, row, bys):
        for by in bys:
            got_own(a, near[by])
            forward_rows(a, row, near[by])

    def cols_on(a, row, bys):
        for by in bys:
            got_own(a, near[by])
            forward_cols(a, row, near[by])

    here = []

    def tiles_of(by):
        j = near[by]
        tile_1(A, j, pl.multiple_of(j * ch, ch), True)
        for other in here:
            tk, tq = jnp.minimum(other, j), jnp.maximum(other, j)
            tile_1(A, tk, pl.multiple_of(tq * ch, ch), False)
        here.append(j)

    rows_on(0, 0, (0,))
    cols_on(1, 4, (0,))
    tiles_of(0)
    rows_on(0, 0, (1, 3))
    cols_on(1, 4, (1, 3))
    tiles_of(1)
    tiles_of(3)
    rows_on(0, 0, (2,))
    cols_on(1, 4, (2,))
    rows_on(2, 2, (0,))
    cols_on(3, 5, (0,))
    tiles_of(2)
    for by in order_in:
        relay(0, 0, near[by])
    for by in order_in:
        got_halo(1, 4, 1, near[by])
    phase_1(DD, 0)
    rows_on(2, 2, (1, 3))
    for by in order_in:
        got_halo(0, 1, 1, near[by])
    phase_1(C, 0)
    rows_on(2, 2, (2,))
    send_part(1, 0, (DD,))
    phase_1(B, 0)
    send_part(0, 0, (B, C))
    cols_on(3, 5, (1, 3))
    phase_1(DD, 1)
    send_part(1, 1, (DD,))
    phase_1(C, 1)
    cols_on(3, 5, (2,))
    for j in near:
        arrived(delta_in.at[j], d_ssem.at[0], d_rsem.at[j])
    deltas[0:1, :] = jnp.concatenate([delta_in[j, 0:1, :] for j in range(n_head)], axis=1)
    send_lse(0)
    phase_1(B, 1)
    send_part(0, 1, (B, C))
    for by in order_in:
        relay(2, 2, near[by])
    for tk in range(half_c):
        row_2(A, tk, tk * ch, half_n - tk * ch, True, False)
    send_lse(1)
    got_lse(1, 0, (DD,))
    for by in order_in:
        got_halo(3, 5, 1, near[by])
    for tk in reversed(range(n_head)):
        row_2(DD, tk, 0, min(tk + 1, half_c) * ch, True, tk == n_head - 1)
    got_lse(1, 1, (DD,))
    for tk in reversed(range(half_c, n_head)):
        row_2(DD, tk, half_n, (tk + 1 - half_c) * ch, False, tk == n_head - 1)
    send_dq(1, 2, 2)
    got_lse(0, 0, (B, C))
    got_lse(0, 1, (B, C))
    for by in order_in:
        got_halo(2, 3, 1, near[by])

    def give_kv(which, j):
        return remote(
            dkv_send.at[which, j], dkv_recv.at[which, j], kv_ssem.at[which, j], kv_rsem.at[which, j],
            along(-1),
        )

    def give_dq(at, j, by):
        return remote(
            dq_send.at[at, j], dq_recv.at[at, j], dq_ssem.at[at, j], dq_rsem.at[at, j], along(by)
        )

    def step_c(step, _):
        tk = lax.rem(me + 1 + step, n_head)
        row_2(C, tk, 0, n, False, False)
        dkv_send[0, tk, :, :] = dka[1, rows(tk), :].astype(BF16)
        dkv_send[1, tk, :, :] = dva[1, rows(tk), :].astype(BF16)
        for which in range(2):
            give_kv(which, tk).start()
        return 0

    lax.fori_loop(0, n_head, step_c, 0)

    def step_ab(step, _):
        tk = lax.rem(me + 1 + step, n_head)
        for at in range(n_head):

            @pl.when(tk == at)
            def _():
                start = max(at * ch, half_n)
                row_2(A, at, start, n - start, at >= half_c, False)

        @pl.when(step < n_head - 1)
        def _():
            row_2(B, tk, 0, n, False, False)

        @pl.when(step == n_head - 1)
        def _():
            def tile(i, _):
                tq = lax.rem(me + 1 + i, n_head)
                cols = pl.ds(pl.multiple_of(tq * ch, ch), ch)
                row_2(B, tk, pl.multiple_of(tq * ch, ch), ch, False, False)
                dq_send[0, tq, :, :] = dqt[1, :, cols].astype(BF16)
                give_dq(0, tq, 1).start()
                return 0

            lax.fori_loop(0, n_head, tile, 0)

        for which in range(2):
            give_kv(which, tk).wait_recv()
        dk = dka[0, rows(tk), :] + dkv_recv[0, tk, :, :].astype(F32)
        dv = dva[0, rows(tk), :] + dkv_recv[1, tk, :, :].astype(F32)
        fin[1, tk, :, :] = (dk * SCALE).astype(BF16)
        fin[2, tk, :, :] = dv.astype(BF16)

        @pl.when(step < n_head - 1)
        def _():
            give(1, tk).start()
            give(2, tk).start()

        return 0

    lax.fori_loop(0, n_head, step_ab, 0)
    keep_out(1).start()
    keep_out(2).start()
    for step in range(n_head):
        j = peer(step + 1)
        for at in (1, 0):
            arrived(dq_recv.at[at, j], dq_ssem.at[at, j], dq_rsem.at[at, j])
        cols = pl.ds(pl.multiple_of(j * ch, ch), ch)
        dq = dqt[0, :, cols] + dq_recv[0, j, :, :].astype(F32) + dq_recv[1, j, :, :].astype(F32)
        fin[0, j, :, :] = (dq.T * SCALE).astype(BF16)
        if step < n_head - 1:
            give(0, j).start()
    keep_out(0).start()

    for j in range(n_head):
        give_dq(0, j, 1).wait_send()
    for which in range(3):
        for step in range(n_head - 1):
            give(which, peer(step + 1)).wait_send()
    for which in range(2):
        for j in range(n_head):
            give_kv(which, j).wait_send()
    for copy in sends:
        copy.wait_send()
    for which in range(3):
        for step in range(n_head):
            j = peer(step)
            arrived(outs[which].at[:, lanes(j)], o_ssem.at[which, j], o_rsem.at[which, j])


def copy_out(*refs):
    ins, outs, buf, sems = refs[:3], refs[3:6], refs[6], refs[7]
    parts = sems.shape[2]
    step = ins[0].shape[0] // parts
    moves = []
    for i in range(3):
        for j in range(parts):
            at = pl.ds(j * step, step)
            moves.append((
                pltpu.make_async_copy(ins[i].at[at], buf.at[i, at], sems.at[0, i, j]),
                pltpu.make_async_copy(buf.at[i, at], outs[i].at[at], sems.at[1, i, j]),
            ))
    for load, _ in moves:
        load.start()
    for load, store in moves:
        load.wait()
        store.start()
    for _, store in moves:
        store.wait()


def solution(mesh):
    n_ctx, n_head = mesh.shape["ctx"], mesh.shape["head"]

    def body(queries, keys, values, output, out_grad, slopes, windows):
        ch, width = queries.shape
        n = ch * n_head
        smem = pl.BlockSpec(memory_space=pltpu.SMEM)
        hbm = pl.BlockSpec(memory_space=pl.ANY)
        dma = pltpu.SemaphoreType.DMA
        vmem = pltpu.VMEM
        out = jax.ShapeDtypeStruct((ch, width), BF16)
        grads = pl.pallas_call(
            functools.partial(kernel, n_ctx, n_head),
            out_shape=[out] * 3,
            in_specs=[smem, smem] + [hbm] * 5,
            out_specs=[hbm] * 3,
            scratch_shapes=[
                vmem((3, n, 2 * D), BF16),
                vmem((2, n, 2 * D), BF16),
                vmem((3, n, D), BF16),
                vmem((2, n, D), BF16),
                vmem((ch, width), BF16),
                vmem((ch, width), BF16),
                vmem((n_head, ch, n + ch), BF16),
                vmem((n_head, ch, n), BF16),
                vmem((n_head, ch, n), BF16),
                vmem((4 * n_head, 2 * SUBS, n), F32),
                vmem((4 * n_head, SUBS, n), F32),
                vmem((3, D, n), F32),
                vmem((2, n, D), F32),
                vmem((2, n, D), F32),
                vmem((n_head, 8, ch), F32),
                vmem((n_head, 8, ch), F32),
                vmem((2, 2, 2, n // 2), F32),
                vmem((2, 2, 2, n // 2), F32),
                vmem((2, 2, n // 2), F32),
                vmem((2, 2, 2, n // 2), F32),
                vmem((3, n), F32),
                vmem((2, n_head, D, ch), BF16),
                vmem((2, n_head, D, ch), BF16),
                vmem((2, n_head, ch, D), BF16),
                vmem((2, n_head, ch, D), BF16),
                vmem((3, n_head, ch, D), BF16),
                dma((4, n_head)),
                dma((4, n_head)),
                dma((6, n_head)),
                dma((6, n_head)),
                dma((n_head,)),
                dma((n_head,)),
                dma((8,)),
                dma((8,)),
                dma((2, n_head)),
                dma((2, n_head)),
                dma((2, n_head)),
                dma((2, n_head)),
                dma((3, n_head)),
                dma((3, n_head)),
                dma((2,)),
            ],
            compiler_params=pltpu.CompilerParams(
                collective_id=0, has_side_effects=True, vmem_limit_bytes=62 << 20
            ),
            cost_estimate=pl.CostEstimate(
                flops=2 * 5 * 3 * n * n * D, bytes_accessed=8 * ch * width * 2,
                transcendentals=3 * n * n,
            ),
        )(slopes, windows, queries, keys, values, output, out_grad)
        return pl.pallas_call(
            copy_out,
            out_shape=[out] * 3,
            in_specs=[hbm] * 3,
            out_specs=[hbm] * 3,
            scratch_shapes=[vmem((3, ch, width), BF16), dma((2, 3, 2))],
        )(*grads)

    split = P(("ctx", "head"), None)
    return jax.shard_map(
        body,
        mesh=mesh,
        in_specs=(split,) * 5 + (P(), P()),
        out_specs=(split,) * 3,
        check_vma=False,
    )
```

```python
import functools
import math

import jax
import jax.numpy as jnp
from jax import lax
from jax.experimental import pallas as pl
from jax.experimental.pallas import tpu as pltpu
from jax.sharding import PartitionSpec as P

D = 128
SCALE = D ** (-0.5)
LOG2E = math.log2(math.e)
TO_LOG2 = SCALE * LOG2E
BIG = 1e30
F32 = jnp.float32
BF16 = jnp.bfloat16
MESH = pl.DeviceIdType.MESH
SUBS = 4
NT_DIMS = (((1,), (1,)), ((), ()))
TN_DIMS = (((0,), (0,)), ((), ()))

A, B, C, DD = range(4)
QSLOT = (0, 1, 1, 2)
KSLOT = (0, 0, 1, 1)


def kernel(
    n_ctx,
    n_head,
    slopes,
    windows,
    q_in,
    k_in,
    v_in,
    o_in,
    g_in,
    dq_out,
    dk_out,
    dv_out,
    qx,
    kx,
    gb,
    vb,
    ov,
    gv,
    p_ad,
    p_b,
    p_c,
    stat,
    ratio,
    dqt,
    dka,
    dva,
    delta_out,
    delta_in,
    part_out,
    part_in,
    ret_out,
    ret_in,
    deltas,
    dq_send,
    dq_recv,
    dkv_send,
    dkv_recv,
    fin,
    x_ssem,
    x_rsem,
    h_ssem,
    h_rsem,
    d_ssem,
    d_rsem,
    s_ssem,
    s_rsem,
    dq_ssem,
    dq_rsem,
    kv_ssem,
    kv_rsem,
    o_ssem,
    o_rsem,
    l_sem,
):
    ch = q_in.shape[0]
    n = n_head * ch
    sub = ch // SUBS
    ctx = lax.axis_index("ctx")
    me = lax.axis_index("head")
    odd = lax.rem(ctx, 2)
    partner = ctx + 1 - 2 * odd

    def along(by):
        return (lax.rem(ctx + by + n_ctx, n_ctx), me)

    def peer(by):
        return lax.rem(me + by, n_head)

    def rows(j):
        return pl.ds(pl.multiple_of(j * ch, ch), ch)

    def lanes(j):
        return pl.ds(pl.multiple_of(j * D, D), D)

    def remote(src, dst, ssem, rsem, device):
        return pltpu.make_async_remote_copy(
            src_ref=src, dst_ref=dst, send_sem=ssem, recv_sem=rsem,
            device_id=device, device_id_type=MESH,
        )

    sends = []

    def send(src, dst, ssem, rsem, device):
        copy = remote(src, dst, ssem, rsem, device)
        copy.start()
        sends.append(copy)

    def arrived(dst, ssem, rsem):
        remote(dst, dst, ssem, rsem, along(0)).wait_recv()

    slope = slopes[me]
    window = windows[me]

    bufs = (qx, kx, gb, vb)
    ins = (q_in, k_in, g_in, v_in)

    def chunk(a, slot, j):
        if a < 2:
            return bufs[a].at[slot, rows(j), 0:D]
        return bufs[a].at[slot, rows(j), :]

    own = []
    for a in range(4):
        copy = pltpu.make_async_copy(ins[a].at[:, lanes(me)], chunk(a, 0, me), x_rsem.at[a, me])
        copy.start()
        own.append(copy)
    copy_o = pltpu.make_async_copy(o_in, ov, l_sem.at[0])
    copy_g = pltpu.make_async_copy(g_in, gv, l_sem.at[1])
    copy_o.start()
    copy_g.start()

    barrier = pltpu.get_barrier_semaphore()
    neighbours = [along(1), along(-1), along(2), along(-2)]
    neighbours += [(ctx, peer(by)) for by in range(1, n_head)]
    for device in neighbours:
        pl.semaphore_signal(barrier, inc=1, device_id=device, device_id_type=MESH)
    pl.semaphore_wait(barrier, len(neighbours))

    first = ((0, 1), (0, 3), (1, 1), (1, 3), (0, 2), (1, 2))
    for a, by in first + ((2, 1), (2, 3), (2, 2), (3, 1), (3, 3), (3, 2)):
        to = peer(by)
        send(ins[a].at[:, lanes(to)], chunk(a, 0, me), x_ssem.at[a, by], x_rsem.at[a, me], (ctx, to))

    lane = lax.broadcasted_iota(jnp.int32, (1, D), 1)
    ones = jnp.broadcast_to(jnp.where(lane < 3, 1.0, 0.0), (ch, D)).astype(BF16)

    def fill(t, _):
        for slot in range(3):
            qx[slot, rows(t), D:] = ones
        pos = (lax.broadcasted_iota(jnp.int32, (ch, D), 0) + t * ch).astype(F32)
        bias = pos * (slope / SCALE)
        high = bias.astype(BF16).astype(F32)
        mid = (bias - high).astype(BF16).astype(F32)
        low = bias - high - mid
        terms = jnp.where(lane == 0, high, jnp.where(lane == 1, mid, jnp.where(lane == 2, low, 0.0)))
        for slot in range(2):
            kx[slot, rows(t), D:] = terms.astype(BF16)
        return 0

    lax.fori_loop(0, n_head, fill, 0)

    for slot in range(2):
        dqt[slot, :, :] = jnp.zeros((D, n), F32)

    copy_o.wait()
    copy_g.wait()
    for h in range(n_head):
        prod = gv[:, h * D:(h + 1) * D].astype(F32) * ov[:, h * D:(h + 1) * D].astype(F32)
        sums = jnp.sum(prod.T, axis=0, keepdims=True)
        delta_out[h, :, :] = jnp.broadcast_to(sums, (8, ch))
    keep = pltpu.make_async_copy(delta_out.at[me], delta_in.at[me], d_rsem.at[me])
    keep.start()
    for by in (1, 3, 2):
        to = peer(by)
        send(delta_out.at[to], delta_in.at[me], d_ssem.at[by], d_rsem.at[me], (ctx, to))

    def got_own(a, j):
        arrived(chunk(a, 0, j), x_ssem.at[a, 0], x_rsem.at[a, j])

    def to_partner(a, row, slot, j):
        return remote(
            chunk(a, slot, j), chunk(a, 1, j), h_ssem.at[row, j], h_rsem.at[row, j], (partner, me)
        )

    def forward_rows(a, row, j):
        send(chunk(a, 0, j), chunk(a, 2, j), h_ssem.at[row, j], h_rsem.at[row, j], along(-2))

        @pl.when(odd == 1)
        def _():
            to_partner(a, row + 1, 0, j).start()

    def forward_cols(a, row, j):
        send(chunk(a, 0, j), chunk(a, 1, j), h_ssem.at[row, j], h_rsem.at[row, j], along(1))

    def relay(a, row, j):
        arrived(chunk(a, 2, j), h_ssem.at[row, j], h_rsem.at[row, j])

        @pl.when(odd == 0)
        def _():
            to_partner(a, row + 1, 2, j).start()

        sends.append(to_partner(a, row + 1, 0, j))

    def got_halo(a, row, slot, j):
        arrived(chunk(a, slot, j), h_ssem.at[row, j], h_rsem.at[row, j])

    order_in = (0, 1, 3, 2)

    def store_p(blk, tk, col, width):
        if blk == A:
            return p_ad.at[tk, :, pl.ds(col + ch, width)]
        if blk == DD:
            return p_ad.at[tk, :, pl.ds(col, width)]
        return (p_b if blk == B else p_c).at[tk, :, pl.ds(col, width)]

    def tile_1(blk, tk, col, masked):
        s = lax.dot_general(
            kx[KSLOT[blk], rows(tk), :], qx[QSLOT[blk], pl.ds(col, ch), :], NT_DIMS,
            preferred_element_type=F32,
        )
        target = store_p(blk, tk, col, ch)
        for u in range(SUBS):
            part = s[u * sub:(u + 1) * sub]
            if masked:
                apart = lax.broadcasted_iota(jnp.int32, (sub, sub), 1) - lax.broadcasted_iota(
                    jnp.int32, (sub, sub), 0
                )
                seen = apart >= 0 if blk == A else apart < window - blk * n
                pieces = [jnp.where(seen, part[:, u * sub:(u + 1) * sub], -BIG)]
                if u > 0:
                    pieces.insert(0, part[:, :u * sub])
                if u < SUBS - 1:
                    pieces.append(part[:, (u + 1) * sub:])
                part = jnp.concatenate(pieces, axis=1)
            top = jnp.max(part, axis=0, keepdims=True)
            p = jnp.exp2((part - top) * TO_LOG2)
            total = jnp.sum(p, axis=0, keepdims=True)
            target[u * sub:(u + 1) * sub, :] = p.astype(BF16)
            stat[blk * n_head + tk, u:u + 1, pl.ds(col, ch)] = top * TO_LOG2
            stat[blk * n_head + tk, SUBS + u:SUBS + u + 1, pl.ds(col, ch)] = total

    half_n = n // 2
    half_c = n_head // 2
    halves_of = [pl.ds(h * half_n, half_n) for h in range(2)]

    def phase_1(blk, h):
        for tk in range(n_head):
            for tq in range(h * half_c, (h + 1) * half_c):
                if blk != DD or tq <= tk:
                    tile_1(blk, tk, tq * ch, tq == tk)

    exists = (
        None,
        ctx + 1 < n_ctx,
        jnp.logical_and(ctx + 1 < n_ctx, ctx >= 1),
        jnp.logical_and(ctx + 2 < n_ctx, ctx >= 1),
    )
    q_part = lax.broadcasted_iota(jnp.int32, (SUBS, half_n), 1) // sub
    k_part = lax.broadcasted_iota(jnp.int32, (SUBS, half_n), 0)

    def seen_row(blk, tk, h):
        apart = q_part + h * half_c * SUBS - (k_part + tk * SUBS)
        if blk == A:
            return apart >= 0
        upto = jnp.where(exists[blk], window - blk * n, -1)
        return jnp.where(apart <= 0, upto, upto - 1) >= 0

    def shift(blk):
        return slope * (-blk * n * LOG2E)

    def tile_tops(blk, tk, h):
        tops = stat[blk * n_head + tk, 0:SUBS, halves_of[h]] + shift(blk)
        return jnp.where(seen_row(blk, tk, h), tops, -BIG)

    def tiles_in(blk, h):
        if blk == A:
            return range((h + 1) * half_c)
        if blk == DD:
            return range(h * half_c, n_head)
        return range(n_head)

    def combine(blks, h, parts):
        tops = [tile_tops(blk, tk, h) for blk in blks for tk in tiles_in(blk, h)]
        tall = functools.reduce(jnp.maximum, tops)
        top = jnp.max(tall, axis=0, keepdims=True)
        for t, _ in parts:
            top = jnp.maximum(top, t)
        total = jnp.zeros((1, half_n), F32)
        for t, v in parts:
            total = total + v * jnp.exp2(t - top)
        several = jnp.zeros((SUBS, half_n), F32)
        i = 0
        for blk in blks:
            for tk in tiles_in(blk, h):
                sums = stat[blk * n_head + tk, SUBS:2 * SUBS, halves_of[h]]
                several = several + jnp.where(
                    seen_row(blk, tk, h), jnp.exp2(tops[i] - top) * sums, 0.0
                )
                i += 1
        return top, total + jnp.sum(several, axis=0, keepdims=True)

    def set_ratio(blk, h, lse):
        for tk in tiles_in(blk, h):
            r = jnp.exp2(tile_tops(blk, tk, h) - lse)
            ratio[blk * n_head + tk, 0:SUBS, halves_of[h]] = jnp.where(seen_row(blk, tk, h), r, 0.0)

    def send_part(at, h, blks):
        top, total = combine(blks, h, ())
        part_out[at, h, 0:1, :] = top
        part_out[at, h, 1:2, :] = total
        i = at * 2 + h
        send(part_out.at[at, h], part_in.at[at, h], s_ssem.at[i], s_rsem.at[i], along(1 + at))

    def send_lse(h):
        for at in range(2):
            i = at * 2 + h
            arrived(part_in.at[at, h], s_ssem.at[i], s_rsem.at[i])
        parts = [(part_in[at, h, 0:1, :], part_in[at, h, 1:2, :]) for at in range(2)]
        top, total = combine((A,), h, parts)
        lse = top + jnp.log(total) * LOG2E
        ret_out[h, 0:1, :] = lse
        ret_out[h, 1:2, :] = deltas[0:1, halves_of[h]]
        for at in (1, 0):
            i = 4 + at * 2 + h
            send(ret_out.at[h], ret_in.at[at, h], s_ssem.at[i], s_rsem.at[i], along(-1 - at))
        set_ratio(A, h, lse)

    def got_lse(at, h, blks):
        i = 4 + at * 2 + h
        arrived(ret_in.at[at, h], s_ssem.at[i], s_rsem.at[i])
        deltas[1 + at:2 + at, halves_of[h]] = ret_in[at, h, 1:2, :]
        for blk in blks:
            set_ratio(blk, h, ret_in[at, h, 0:1, :])

    def row_2(blk, tk, col, width, first_k, first_q):
        qs, ks = QSLOT[blk], KSLOT[blk]
        cols = pl.ds(col, width)
        dp = lax.dot_general(
            vb[ks, rows(tk), :], gb[qs, cols, :], NT_DIMS, preferred_element_type=F32
        )
        delta_row = deltas[qs:qs + 1, cols]
        source = store_p(blk, tk, col, width)
        halves = []
        scores = []
        for u in range(SUBS):
            r = ratio[blk * n_head + tk, u:u + 1, cols].astype(BF16)
            half = source[u * sub:(u + 1) * sub, :] * r
            halves.append(half)
            scores.append(half * (dp[u * sub:(u + 1) * sub] - delta_row).astype(BF16))
        half = jnp.concatenate(halves, axis=0)
        score = jnp.concatenate(scores, axis=0)
        dv = jnp.dot(half, gb[qs, cols, :], preferred_element_type=F32)
        dk = jnp.dot(score, qx[qs, cols, 0:D], preferred_element_type=F32)
        dq = lax.dot_general(kx[ks, rows(tk), 0:D], score, TN_DIMS, preferred_element_type=F32)
        if first_k:
            dva[ks, rows(tk), :] = dv
            dka[ks, rows(tk), :] = dk
        else:
            dva[ks, rows(tk), :] += dv
            dka[ks, rows(tk), :] += dk
        if first_q:
            dqt[qs, :, cols] = dq
        else:
            dqt[qs, :, cols] += dq

    def send_dq(at, slot, by):
        for step in range(n_head):
            j = peer(step + 1)
            cols = pl.ds(pl.multiple_of(j * ch, ch), ch)
            dq_send[at, j, :, :] = dqt[slot, :, cols].astype(BF16)
            send(
                dq_send.at[at, j], dq_recv.at[at, j], dq_ssem.at[at, j], dq_rsem.at[at, j], along(by)
            )

    outs = (dq_out, dk_out, dv_out)

    def give(which, j):
        return remote(
            fin.at[which, j], outs[which].at[:, lanes(me)], o_ssem.at[which, j], o_rsem.at[which, me],
            (ctx, j),
        )

    def keep_out(which):
        return pltpu.make_async_copy(
            fin.at[which, me], outs[which].at[:, lanes(me)], o_rsem.at[which, me]
        )

    near = [peer(by) for by in range(n_head)]

    def rows_on(a, row, bys):
        for by in bys:
            got_own(a, near[by])
            forward_rows(a, row, near[by])

    def cols_on(a, row, bys):
        for by in bys:
            got_own(a, near[by])
            forward_cols(a, row, near[by])

    here = []

    def tiles_of(by):
        j = near[by]
        tile_1(A, j, pl.multiple_of(j * ch, ch), True)
        for other in here:
            tk, tq = jnp.minimum(other, j), jnp.maximum(other, j)
            tile_1(A, tk, pl.multiple_of(tq * ch, ch), False)
        here.append(j)

    rows_on(0, 0, (0,))
    cols_on(1, 4, (0,))
    tiles_of(0)
    rows_on(0, 0, (1, 3))
    cols_on(1, 4, (1, 3))
    tiles_of(1)
    tiles_of(3)
    rows_on(0, 0, (2,))
    cols_on(1, 4, (2,))
    rows_on(2, 2, (0,))
    cols_on(3, 5, (0,))
    tiles_of(2)
    for by in order_in:
        relay(0, 0, near[by])
    for by in order_in:
        got_halo(1, 4, 1, near[by])
    phase_1(DD, 0)
    rows_on(2, 2, (1, 3))
    for by in order_in:
        got_halo(0, 1, 1, near[by])
    phase_1(C, 0)
    rows_on(2, 2, (2,))
    send_part(1, 0, (DD,))
    phase_1(B, 0)
    send_part(0, 0, (B, C))
    cols_on(3, 5, (1, 3))
    phase_1(DD, 1)
    send_part(1, 1, (DD,))
    phase_1(C, 1)
    cols_on(3, 5, (2,))
    for j in near:
        arrived(delta_in.at[j], d_ssem.at[0], d_rsem.at[j])
    deltas[0:1, :] = jnp.concatenate([delta_in[j, 0:1, :] for j in range(n_head)], axis=1)
    send_lse(0)
    phase_1(B, 1)
    send_part(0, 1, (B, C))
    for by in order_in:
        relay(2, 2, near[by])
    for tk in range(half_c):
        row_2(A, tk, tk * ch, half_n - tk * ch, True, False)
    send_lse(1)
    got_lse(1, 0, (DD,))
    for by in order_in:
        got_halo(3, 5, 1, near[by])
    for tk in reversed(range(n_head)):
        row_2(DD, tk, 0, min(tk + 1, half_c) * ch, True, tk == n_head - 1)
    got_lse(1, 1, (DD,))
    for tk in reversed(range(half_c, n_head)):
        row_2(DD, tk, half_n, (tk + 1 - half_c) * ch, False, tk == n_head - 1)
    send_dq(1, 2, 2)
    got_lse(0, 0, (B, C))
    got_lse(0, 1, (B, C))
    for by in order_in:
        got_halo(2, 3, 1, near[by])

    def give_kv(which, j):
        return remote(
            dkv_send.at[which, j], dkv_recv.at[which, j], kv_ssem.at[which, j], kv_rsem.at[which, j],
            along(-1),
        )

    def give_dq(at, j, by):
        return remote(
            dq_send.at[at, j], dq_recv.at[at, j], dq_ssem.at[at, j], dq_rsem.at[at, j], along(by)
        )

    def step_c(step, _):
        tk = lax.rem(me + 1 + step, n_head)
        row_2(C, tk, 0, n, False, False)
        dkv_send[0, tk, :, :] = dka[1, rows(tk), :].astype(BF16)
        dkv_send[1, tk, :, :] = dva[1, rows(tk), :].astype(BF16)
        for which in range(2):
            give_kv(which, tk).start()
        return 0

    lax.fori_loop(0, n_head, step_c, 0)

    def finish_kv(tk):
        for which in range(2):
            give_kv(which, tk).wait_recv()
        dk = dka[0, rows(tk), :] + dkv_recv[0, tk, :, :].astype(F32)
        dv = dva[0, rows(tk), :] + dkv_recv[1, tk, :, :].astype(F32)
        fin[1, tk, :, :] = (dk * SCALE).astype(BF16)
        fin[2, tk, :, :] = dv.astype(BF16)

    def step_ab(step, _):
        tk = lax.rem(me + 1 + step, n_head)
        for at in range(n_head):

            @pl.when(tk == at)
            def _():
                start = max(at * ch, half_n)
                row_2(A, at, start, n - start, at >= half_c, False)

        @pl.when(step < n_head - 1)
        def _():
            row_2(B, tk, 0, n, False, False)

        @pl.when(step == n_head - 1)
        def _():
            def tile(i, _):
                tq = lax.rem(me + 1 + i, n_head)
                cols = pl.ds(pl.multiple_of(tq * ch, ch), ch)
                row_2(B, tk, pl.multiple_of(tq * ch, ch), ch, False, False)
                dq_send[0, tq, :, :] = dqt[1, :, cols].astype(BF16)
                give_dq(0, tq, 1).start()
                return 0

            lax.fori_loop(0, n_head, tile, 0)

        @pl.when(step < n_head - 1)
        def _():
            finish_kv(tk)
            give(1, tk).start()
            give(2, tk).start()

        return 0

    lax.fori_loop(0, n_head, step_ab, 0)
    for step in range(n_head):
        j = peer(step + 1)
        for at in (1, 0):
            arrived(dq_recv.at[at, j], dq_ssem.at[at, j], dq_rsem.at[at, j])
        cols = pl.ds(pl.multiple_of(j * ch, ch), ch)
        dq = dqt[0, :, cols] + dq_recv[0, j, :, :].astype(F32) + dq_recv[1, j, :, :].astype(F32)
        fin[0, j, :, :] = (dq.T * SCALE).astype(BF16)
        if step < n_head - 1:
            give(0, j).start()
    keep_out(0).start()
    finish_kv(me)
    keep_out(1).start()
    keep_out(2).start()

    for j in range(n_head):
        give_dq(0, j, 1).wait_send()
    for which in range(3):
        for step in range(n_head - 1):
            give(which, peer(step + 1)).wait_send()
    for which in range(2):
        for j in range(n_head):
            give_kv(which, j).wait_send()
    for copy in sends:
        copy.wait_send()
    for which in range(3):
        for step in range(n_head):
            j = peer(step)
            arrived(outs[which].at[:, lanes(j)], o_ssem.at[which, j], o_rsem.at[which, j])


def copy_out(*refs):
    ins, outs, buf, sems = refs[:3], refs[3:6], refs[6], refs[7]
    parts = sems.shape[2]
    step = ins[0].shape[0] // parts
    moves = []
    for i in range(3):
        for j in range(parts):
            at = pl.ds(j * step, step)
            moves.append((
                pltpu.make_async_copy(ins[i].at[at], buf.at[i, at], sems.at[0, i, j]),
                pltpu.make_async_copy(buf.at[i, at], outs[i].at[at], sems.at[1, i, j]),
            ))
    for load, _ in moves:
        load.start()
    for load, store in moves:
        load.wait()
        store.start()
    for _, store in moves:
        store.wait()


def solution(mesh):
    n_ctx, n_head = mesh.shape["ctx"], mesh.shape["head"]

    def body(queries, keys, values, output, out_grad, slopes, windows):
        ch, width = queries.shape
        n = ch * n_head
        smem = pl.BlockSpec(memory_space=pltpu.SMEM)
        hbm = pl.BlockSpec(memory_space=pl.ANY)
        dma = pltpu.SemaphoreType.DMA
        vmem = pltpu.VMEM
        out = jax.ShapeDtypeStruct((ch, width), BF16)
        grads = pl.pallas_call(
            functools.partial(kernel, n_ctx, n_head),
            out_shape=[out] * 3,
            in_specs=[smem, smem] + [hbm] * 5,
            out_specs=[hbm] * 3,
            scratch_shapes=[
                vmem((3, n, 2 * D), BF16),
                vmem((2, n, 2 * D), BF16),
                vmem((3, n, D), BF16),
                vmem((2, n, D), BF16),
                vmem((ch, width), BF16),
                vmem((ch, width), BF16),
                vmem((n_head, ch, n + ch), BF16),
                vmem((n_head, ch, n), BF16),
                vmem((n_head, ch, n), BF16),
                vmem((4 * n_head, 2 * SUBS, n), F32),
                vmem((4 * n_head, SUBS, n), F32),
                vmem((3, D, n), F32),
                vmem((2, n, D), F32),
                vmem((2, n, D), F32),
                vmem((n_head, 8, ch), F32),
                vmem((n_head, 8, ch), F32),
                vmem((2, 2, 2, n // 2), F32),
                vmem((2, 2, 2, n // 2), F32),
                vmem((2, 2, n // 2), F32),
                vmem((2, 2, 2, n // 2), F32),
                vmem((3, n), F32),
                vmem((2, n_head, D, ch), BF16),
                vmem((2, n_head, D, ch), BF16),
                vmem((2, n_head, ch, D), BF16),
                vmem((2, n_head, ch, D), BF16),
                vmem((3, n_head, ch, D), BF16),
                dma((4, n_head)),
                dma((4, n_head)),
                dma((6, n_head)),
                dma((6, n_head)),
                dma((n_head,)),
                dma((n_head,)),
                dma((8,)),
                dma((8,)),
                dma((2, n_head)),
                dma((2, n_head)),
                dma((2, n_head)),
                dma((2, n_head)),
                dma((3, n_head)),
                dma((3, n_head)),
                dma((2,)),
            ],
            compiler_params=pltpu.CompilerParams(
                collective_id=0, has_side_effects=True, vmem_limit_bytes=62 << 20
            ),
            cost_estimate=pl.CostEstimate(
                flops=2 * 5 * 3 * n * n * D, bytes_accessed=8 * ch * width * 2,
                transcendentals=3 * n * n,
            ),
        )(slopes, windows, queries, keys, values, output, out_grad)
        return pl.pallas_call(
            copy_out,
            out_shape=[out] * 3,
            in_specs=[hbm] * 3,
            out_specs=[hbm] * 3,
            scratch_shapes=[vmem((3, ch, width), BF16), dma((2, 3, 2))],
        )(*grads)

    split = P(("ctx", "head"), None)
    return jax.shard_map(
        body,
        mesh=mesh,
        in_specs=(split,) * 5 + (P(), P()),
        out_specs=(split,) * 3,
        check_vma=False,
    )
```
